32 devices in a mesh: gx: 4 (over x, core), gy: 8 (over z, y).
Axes of the slice: x: 2, y: 2, z: 4, core: 2. Of those that a mesh axis runs over, the one named last changes fastest.
Arguments:
- off_state: float32 [5, 128, 128, 256], P(None, 'gx', 'gy'), may hold values from -0.9 to 3, as said below
- near_state: float32 [96, 5, 8, 64, 128], P(('gx', 'gy')), may hold values from -0.9 to 3, as said below
- near_metric: float32 [96, 3, 8, 64, 128], P(('gx', 'gy')), may hold values from 0.5 to 1.1
- slot_block: int32 [96], P(('gx', 'gy')), may hold values from -1 to 63, as said below
- block_faces: int32 [64, 2], replicated, may hold values from 0 to 63, as said below
- fringe_in: int32 [3, 256], P(None, ('gx', 'gy')), may hold values from 0 to 23, as said below
- fringe_in_maps: bfloat16 [256, 128, 128], P(('gx', 'gy')), may hold values from 0 to 1
- fringe_out: int32 [3, 256], P(None, ('gx', 'gy')), may hold values from 0 to 23, as said below
- fringe_out_maps: bfloat16 [256, 128, 128], P(('gx', 'gy')), may hold values from 0 to 1
Outputs:
- off_next: float32 [5, 128, 128, 256], P(None, 'gx', 'gy')
- near_next: float32 [96, 5, 8, 64, 128], P(('gx', 'gy'))
The draws below stay inside these ranges and needn't reach their ends.
Inputs may be any that keep to these rules, and one draw needn't show every extreme that they name: `off_state`: component 0 (density) lies within 0.8 to 1.2, components 1 to 3 within -0.9 to 0.9, component 4 within 2 to 3. `near_state`: component 0 (density) lies within 0.8 to 1.2, components 1 to 3 within -0.9 to 0.9, component 4 within 2 to 3, in empty slots too. `slot_block`: entry 3 * d + s is the block in slot s of device d (devices in gx+gy order). A device's occupied slots come first and it holds at least one block; every block is in exactly one slot; the blocks of gx row r are numbered from r * 2 * 8 and held in that row; the devices at gy and gy + 4 of one row hold 4 blocks together. `block_faces`: row b gives the block across b's lower and upper face around the body; they agree (b is the lower neighbour of its upper neighbour) and lie in b's gx row. `fringe_in`: column 8 * d + k is row k of device d: entry 0 a near-body tile of d in an occupied slot, entry 1 the gy index of the receiving device in d's gx row, entry 2 one of its off-body tiles. Every off-body tile is replaced at most once; every device receives exactly 8 rows, and sends exactly 1 row to each of 8 devices. `fringe_out`: column 8 * d + k is row k of device d: entry 0 an off-body tile of d, entry 1 the gy index of the receiving device in d's gx row, entry 2 a near-body tile of that device in an occupied slot. Every near-body tile is replaced at most once; every device receives exactly 8 rows, and sends exactly 1 row to each of 8 devices.
All inputs are finite; a program needn't handle non-finite values.
Results may differ from the reference program's by a relative error of at most 0.0014.
The reference program's roundings to bfloat16 on the way count: a program that leaves them out, or rounds other values in their place, can miss the bound.
Values may be sent and summed in bfloat16 or wider, within the bound.
No kernel may reach another device: no remote copies, remote signals or barrier semaphores. Data moves between devices by JAX's collectives and lax.ppermute only.
A program may use at most 384 MiB of HBM per device.

```python
import math
import jax
import jax.numpy as jnp
from jax import lax

CX = 32
CY = 16
NZ = 256
TW = 8
TL = 128
NJ = 64
BLK_DEV = 2
FR_DEV = 8
FCAP = 1
NX = 128
NY = 128
BCAP = 3
SLOTS = 96
TPB = 8
NT_OFF = 16
N_GX = 4
N_GY = 8
DEVICES = 32


def alternating(cells):
    dimensions = len(cells)
    index_sum = jnp.zeros((), jnp.int32)
    for axis_number in range(dimensions - 3, dimensions):
        view_shape = [1] * dimensions
        view_shape[axis_number] = cells[axis_number]
        index_sum = index_sum + jnp.arange(cells[axis_number], dtype=jnp.int32).reshape(view_shape)
    return 1.0 - 2.0 * (index_sum % 2).astype(jnp.float32)


def flow_fields(key, cells):
    density_key, momentum_key, energy_key = jax.random.split(key, 3)
    lone_member = (1,) + cells
    parity_sign = alternating(cells)[None]
    density = 0.8 + 0.4 * jax.random.uniform(density_key, lone_member)
    magnitude = jax.random.uniform(momentum_key, (3,) + cells, minval=0.2, maxval=0.8)
    energy = 2.0 + jax.random.uniform(energy_key, lone_member)
    momentum = parity_sign * magnitude
    return jnp.concatenate([density, momentum, energy], axis=0).astype(jnp.float32)


def draw_off_state(key, part):
    return flow_fields(jax.random.fold_in(key, 1), (NX, NY, NZ))


def draw_near_state(key, part):
    fields = flow_fields(jax.random.fold_in(key, 2), (SLOTS, TW, NJ, TL))
    return jnp.moveaxis(fields, 0, 1)


def interpolation_maps(key, row_total):
    scores = 3.0 * jax.random.normal(key, (row_total, TL, TL))
    weights = jax.nn.softmax(scores, axis=-1)
    return (0.6 * jnp.eye(TL, dtype=jnp.float32) + 0.4 * weights).astype(jnp.bfloat16)


def draw_fringe_in_maps(key, part):
    return interpolation_maps(jax.random.fold_in(key, 3), DEVICES * FR_DEV)


def draw_fringe_out_maps(key, part):
    return interpolation_maps(jax.random.fold_in(key, 4), DEVICES * FR_DEV)


def placement(key):
    half_axis = N_GY // 2
    row_keys = jax.random.split(jax.random.fold_in(key, 11), N_GX)
    pair_load = jax.random.randint(jax.random.fold_in(key, 12), (N_GX, half_axis), 1, 2 * BLK_DEV)
    heavy_pair = jax.random.randint(jax.random.fold_in(key, 13), (N_GX, 1), 0, half_axis)
    pair_load = jnp.where(jnp.arange(half_axis)[None, :] == heavy_pair, 2 * BLK_DEV - 1, pair_load)
    row_order = jax.vmap(lambda row_key: jax.random.permutation(row_key, BLK_DEV * N_GY))(row_keys)
    column = jnp.arange(N_GY)
    pair_index = column % half_axis
    upper_half = (column >= half_axis)[None, :]
    lower_load = pair_load[:, pair_index]
    device_load = jnp.where(upper_half, 2 * BLK_DEV - lower_load, lower_load)
    first_seat = 2 * BLK_DEV * pair_index[None, :] + jnp.where(upper_half, lower_load, 0)
    seat_index = jnp.arange(BCAP)
    position = jnp.clip(first_seat[:, :, None] + seat_index[None, None, :], 0, BLK_DEV * N_GY - 1)
    local_block = jnp.take_along_axis(row_order, position.reshape(N_GX, -1), axis=1).reshape(N_GX, N_GY, BCAP)
    blocks = jnp.arange(N_GX)[:, None, None] * (BLK_DEV * N_GY) + local_block
    seats = jnp.where(seat_index[None, None, :] < device_load[:, :, None], blocks, -1)
    return (seats.astype(jnp.int32), device_load.astype(jnp.int32))


def draw_slot_block(key, part):
    seats, device_load = placement(key)
    return seats.reshape(-1)


def draw_block_faces(key, part):
    row_keys = jax.random.split(jax.random.fold_in(key, 21), N_GX)
    length = BLK_DEV * N_GY
    cycle = jax.vmap(lambda row_key: jax.random.permutation(row_key, length))(row_keys)
    successor = jnp.roll(cycle, -1, axis=1)
    predecessor = jnp.roll(cycle, 1, axis=1)
    row_base = jnp.arange(N_GX)[:, None] * length
    row_number = jnp.arange(N_GX)[:, None]
    higher = jnp.zeros((N_GX, length), jnp.int32).at[row_number, cycle].set(successor + row_base)
    lower = jnp.zeros((N_GX, length), jnp.int32).at[row_number, cycle].set(predecessor + row_base)
    return jnp.stack([lower.reshape(-1), higher.reshape(-1)], axis=1).astype(jnp.int32)


def fringe_table(key, salt, donor_count, receiver_count, pool):
    base_key = jax.random.fold_in(key, salt)
    loop_keys = jax.random.split(jax.random.fold_in(base_key, 1), N_GX)
    loop = jax.vmap(lambda row_key: jax.random.permutation(row_key, N_GY))(loop_keys)
    loop_place = jnp.argsort(loop, axis=1)
    offset_keys = jax.random.split(jax.random.fold_in(base_key, 2), N_GX)
    offsets = jax.vmap(lambda row_key: jax.random.permutation(row_key, N_GY))(offset_keys)[:, :FR_DEV // FCAP]
    step_shift = jnp.repeat(offsets, FCAP, axis=1)
    target_place = (loop_place[:, :, None] + step_shift[:, None, :]) % N_GY
    receiver = jnp.take_along_axis(loop, target_place.reshape(N_GX, -1), axis=1).reshape(N_GX, N_GY, FR_DEV)
    tile_keys = jax.random.split(jax.random.fold_in(base_key, 3), N_GX * N_GY)
    scores = jax.vmap(lambda tile_key: jax.random.permutation(tile_key, pool))(tile_keys).reshape(N_GX, N_GY, pool)
    unusable = (jnp.arange(pool)[None, None, :] >= receiver_count[:, :, None]).astype(jnp.int32)
    ranked = jnp.argsort(scores + unusable * pool, axis=2)[:, :, :FR_DEV]
    receiver_tile = jnp.take_along_axis(ranked, receiver, axis=1)
    donor_tile = jax.random.randint(jax.random.fold_in(base_key, 4), (N_GX, N_GY, FR_DEV), 0, donor_count[:, :, None])
    return jnp.stack([donor_tile.reshape(-1), receiver.reshape(-1), receiver_tile.reshape(-1)], axis=0).astype(jnp.int32)


def draw_fringe_in(key, part):
    seats, device_load = placement(key)
    every_tile = jnp.full((N_GX, N_GY), NT_OFF, jnp.int32)
    return fringe_table(key, 31, device_load * TPB, every_tile, NT_OFF)


def draw_fringe_out(key, part):
    seats, device_load = placement(key)
    every_tile = jnp.full((N_GX, N_GY), NT_OFF, jnp.int32)
    return fringe_table(key, 41, every_tile, device_load * TPB, BCAP * TPB)


def block_levels(stream_key, dims, cuts, smallest, largest):
    factor_of = 1.0
    for dim, shards_of in cuts:
        heights = jax.random.uniform(jax.random.fold_in(jax.random.fold_in(stream_key, 6), dim), (shards_of,), jnp.float32, smallest / len(cuts), largest / len(cuts))
        factor_of = factor_of * jnp.repeat(jnp.exp(heights), dims[dim] // shards_of).reshape((-1,) + (1,) * (len(dims) - 1 - dim))
    return factor_of


def setup_inputs(seed: int = 0) -> dict:
    arg_keys = jax.random.split(jax.random.key(seed), 10)
    return {
        "off_state": draw_off_state(jax.random.fold_in(arg_keys[9], 71), 0),
        "near_state": draw_near_state(jax.random.fold_in(arg_keys[9], 71), 0),
        "near_metric": jnp.clip(jnp.exp(math.log(1.1) - 0.7884574 * jax.random.uniform(arg_keys[2], (SLOTS, 3, TW, NJ, TL), jnp.float32) ** block_levels(arg_keys[2], (SLOTS, 3, TW, NJ, TL), ((0, 32),), -0.2, 0.2)), 0.5, 1.1),
        "slot_block": draw_slot_block(jax.random.fold_in(arg_keys[9], 71), 0),
        "block_faces": draw_block_faces(jax.random.fold_in(arg_keys[9], 71), 0),
        "fringe_in": draw_fringe_in(jax.random.fold_in(arg_keys[9], 71), 0),
        "fringe_in_maps": draw_fringe_in_maps(jax.random.fold_in(arg_keys[9], 71), 0),
        "fringe_out": draw_fringe_out(jax.random.fold_in(arg_keys[9], 71), 0),
        "fringe_out_maps": draw_fringe_out_maps(jax.random.fold_in(arg_keys[9], 71), 0),
    }


HEAT_RATIO = 1.4
VISCOSITY = 0.8
CONDUCTION = 1.12
TIME_STEP = 0.1
WALL_SIGN = (1.0, -1.0, -1.0, -1.0, 1.0)
QUIET_STATE = (1.0, 0.0, 0.0, 0.0, 2.5)


def shifted(values, direction, offset):
    leading = values.ndim - 3
    selector = [slice(None)] * leading
    for spatial in range(3):
        extent = values.shape[leading + spatial]
        if spatial == direction:
            selector.append(slice(1 + offset, extent - 1 + offset))
        else:
            selector.append(slice(1, extent - 1))
    return values[tuple(selector)]


def member(values, number):
    return values[..., number, :, :, :]


def residual(padded, metric):
    density = member(padded, 0)
    reciprocal_mass_per_volume = 1.0 / density
    fluid_speed_vector = [member(padded, 1 + direction) * reciprocal_mass_per_volume for direction in range(3)]
    motion_work_share = 0.5 * (fluid_speed_vector[0] * fluid_speed_vector[0] + fluid_speed_vector[1] * fluid_speed_vector[1] + fluid_speed_vector[2] * fluid_speed_vector[2])
    energy = member(padded, 4)
    normal_stress_level = (HEAT_RATIO - 1.0) * (energy - density * motion_work_share)
    thermal_level = normal_stress_level * reciprocal_mass_per_volume
    viscous_contribution = jnp.stack([fluid_speed_vector[0], fluid_speed_vector[1], fluid_speed_vector[2], motion_work_share, thermal_level], axis=-4)
    middle = shifted(viscous_contribution, 0, 0)
    summed = None
    for direction in range(3):
        momentum = member(padded, 1 + direction)
        pieces = [momentum, momentum * fluid_speed_vector[0], momentum * fluid_speed_vector[1], momentum * fluid_speed_vector[2],
                  (energy + normal_stress_level) * fluid_speed_vector[direction]]
        pieces[1 + direction] = pieces[1 + direction] + normal_stress_level
        fluxes = jnp.stack(pieces, axis=-4)
        difference = shifted(fluxes, direction, 1) - shifted(fluxes, direction, -1)
        second = shifted(viscous_contribution, direction, 1) + shifted(viscous_contribution, direction, -1) - 2.0 * middle
        viscous = jnp.stack([jnp.zeros_like(member(second, 0)), VISCOSITY * member(second, 0),
                             VISCOSITY * member(second, 1), VISCOSITY * member(second, 2),
                             VISCOSITY * member(second, 3) + CONDUCTION * member(second, 4)], axis=-4)
        if metric is None:
            contrib = viscous - 0.5 * difference
        else:
            spacing = jnp.expand_dims(member(metric, direction), -4)
            contrib = spacing * spacing * viscous - 0.5 * spacing * difference
        summed = contrib if summed is None else summed + contrib
    return summed


def runge_kutta(initial, rate_of):
    section_one = initial + TIME_STEP * rate_of(initial)
    section_two = 0.75 * initial + 0.25 * (section_one + TIME_STEP * rate_of(section_one))
    return (1.0 / 3.0) * initial + (2.0 / 3.0) * (section_two + TIME_STEP * rate_of(section_two))


def frame_near(current, ghost_low, upper_ghost_cells):
    joined = jnp.concatenate([ghost_low, current, upper_ghost_cells], axis=3)
    wall_sign = jnp.array(WALL_SIGN, jnp.float32).reshape(5, 1, 1, 1)
    joined = jnp.concatenate([joined[:, :, 0:1] * wall_sign, joined, joined[:, :, -1:]], axis=2)
    return jnp.concatenate([joined[..., 0:1], joined, joined[..., -1:]], axis=4)


def interpolate(donors, tile_maps):
    rounded = lax.optimization_barrier(donors.astype(jnp.bfloat16)).astype(jnp.float32)
    tile_lines = rounded.reshape(donors.shape[0], -1, tile_maps.shape[-1])
    mixed_rows = jnp.einsum("rkl,rlm->rkm", tile_lines, tile_maps.astype(jnp.float32),
                            precision=lax.Precision.HIGHEST)
    result = lax.optimization_barrier(mixed_rows.astype(jnp.bfloat16)).astype(jnp.float32)
    return result.reshape(donors.shape[0], -1)


def reference(off_state, near_state, near_metric, slot_block, block_faces, fringe_in, fringe_in_maps,
              fringe_out, fringe_out_maps):
    occupied = slot_block >= 0
    quiet_state = jnp.array(QUIET_STATE, jnp.float32).reshape(1, 5, 1, 1, 1)
    near_filled = jnp.where(occupied[:, None, None, None, None], near_state, quiet_state)
    tile_count = (CX // TW) * (CY // TW) * (NZ // TL)
    per_slot = NJ // TW
    tiles_off = off_state.reshape(5, N_GX, CX // TW, TW, N_GY, CY // TW, TW, NZ // TL, TL)
    tiles_off = tiles_off.transpose(1, 4, 2, 5, 7, 0, 3, 6, 8).reshape(N_GX * N_GY * tile_count, -1)
    tiles_near = near_filled.reshape(SLOTS, 5, TW, per_slot, TW, TL)
    tiles_near = tiles_near.transpose(0, 3, 1, 2, 4, 5).reshape(SLOTS * per_slot, -1)
    device = jnp.arange(N_GX * N_GY * FR_DEV, dtype=jnp.int32) // FR_DEV
    row_first = (device // N_GY) * N_GY
    donor_in = device * (BCAP * per_slot) + fringe_in[0]
    target_in = (row_first + fringe_in[1]) * tile_count + fringe_in[2]
    donor_out = device * tile_count + fringe_out[0]
    target_out = (row_first + fringe_out[1]) * (BCAP * per_slot) + fringe_out[2]
    values_in = interpolate(tiles_near[donor_in], fringe_in_maps)
    values_out = interpolate(tiles_off[donor_out], fringe_out_maps)
    tiles_off = tiles_off.at[target_in].set(values_in)
    marks_off = jnp.zeros((N_GX * N_GY * tile_count,), jnp.float32).at[target_in].set(1.0)
    tiles_near = tiles_near.at[target_out].set(values_out)
    marks_near = jnp.zeros((SLOTS * per_slot,), jnp.float32).at[target_out].set(1.0)

    off_start = tiles_off.reshape(N_GX, N_GY, CX // TW, CY // TW, NZ // TL, 5, TW, TW, TL)
    off_start = off_start.transpose(5, 0, 2, 6, 1, 3, 7, 4, 8).reshape(5, NX, NY, NZ)
    tile_grid = marks_off.reshape(N_GX, N_GY, CX // TW, CY // TW, NZ // TL).transpose(0, 2, 1, 3, 4)
    tile_grid = tile_grid[:, :, None, :, :, None, :, None]
    spread = jnp.broadcast_to(tile_grid, (N_GX, CX // TW, TW, N_GY, CY // TW, TW, NZ // TL, TL))
    hold_off = 1.0 - spread.reshape(NX, NY, NZ)

    def off_rate(fields):
        padded = jnp.pad(fields, ((0, 0), (1, 1), (1, 1), (1, 1)), mode="wrap")

        def slab_rate(position):
            return residual(lax.dynamic_slice_in_dim(padded, position * CX, CX + 2, axis=1), None)

        slab_rates = lax.map(slab_rate, jnp.arange(N_GX, dtype=jnp.int32))
        return slab_rates.transpose(1, 0, 2, 3, 4).reshape(5, NX, NY, NZ) * hold_off

    off_next = runge_kutta(off_start, off_rate)

    near_start = tiles_near.reshape(SLOTS, per_slot, 5, TW, TW, TL)
    near_start = near_start.transpose(0, 2, 3, 1, 4, 5).reshape(SLOTS, 5, TW, NJ, TL)
    hold_near = 1.0 - jnp.repeat(marks_near.reshape(SLOTS, per_slot), TW, axis=1)[:, None, None, :, None]
    row_slots = N_GY * BCAP
    row_blocks = N_GY * BLK_DEV

    def line_advance(bundle):
        fields, metric, hold_mask, block_ids, row_number = bundle
        present = block_ids >= 0
        local_block = jnp.where(present, block_ids - row_number * row_blocks, row_blocks)
        slot_of_block = jnp.zeros((row_blocks,), jnp.int32).at[local_block].set(
            jnp.arange(row_slots, dtype=jnp.int32), mode="drop")
        guarded_block = jnp.where(present, block_ids, 0)
        lower_local = jnp.clip(block_faces[guarded_block, 0] - row_number * row_blocks, 0, row_blocks - 1)
        upper_local = jnp.clip(block_faces[guarded_block, 1] - row_number * row_blocks, 0, row_blocks - 1)
        lower_slot = slot_of_block[lower_local]
        upper_slot = slot_of_block[upper_local]

        def near_rate(current):
            ghost_low = current[lower_slot, :, :, NJ - 1:NJ, :]
            upper_ghost_cells = current[upper_slot, :, :, 0:1, :]
            return residual(frame_near(current, ghost_low, upper_ghost_cells), metric) * hold_mask

        return runge_kutta(fields, near_rate)

    bundles = (near_start.reshape(N_GX, row_slots, 5, TW, NJ, TL),
               near_metric.reshape(N_GX, row_slots, 3, TW, NJ, TL),
               hold_near.reshape(N_GX, row_slots, 1, 1, NJ, 1),
               slot_block.reshape(N_GX, row_slots),
               jnp.arange(N_GX, dtype=jnp.int32))
    stepped = lax.map(line_advance, bundles).reshape(SLOTS, 5, TW, NJ, TL)
    near_next = jnp.where(occupied[:, None, None, None, None], stepped, 0.0)
    return off_next, near_next
```

```python
import functools

import jax
import jax.numpy as jnp
from jax import lax
from jax.experimental import pallas as pl
from jax.experimental.pallas import tpu as pltpu
from jax.sharding import PartitionSpec as P

TW = 8
TL = 128
DEPTH = 3
RING = 8
META = 16
FIELDS = 5
HEAT_RATIO = 1.4
VISCOSITY = 0.8
CONDUCTION = 1.12
TIME_STEP = 0.1
QUIET_STATE = (1.0, 0.0, 0.0, 0.0, 2.5)
CENTRE = (1.0, 0.0, 0.0, 0.0, 2.5, 0.0)
SECTIONS = ((0.0, 1.0), (0.75, 0.25), (1.0 / 3.0, 2.0 / 3.0))
FACE_LAYERS = FIELDS * DEPTH + 3 * (DEPTH - 1) + 1
FACE_ROWS = FACE_LAYERS * TW
LAG = 2
RINGS = 4
VMEM_MIB = 56
FRONT = 6

VMEM = pltpu.VMEM
SMEM = pltpu.SMEM


def vmem_spec():
    return pl.BlockSpec(memory_space=VMEM)


def smem_spec():
    return pl.BlockSpec(memory_space=SMEM)


def any_spec():
    return pl.BlockSpec(memory_space=pl.ANY)


def params(mebibytes):
    return pltpu.CompilerParams(vmem_limit_bytes=mebibytes * 1024 * 1024)


def cost(flops, moved):
    return pl.CostEstimate(flops=int(flops), bytes_accessed=int(moved), transcendentals=0)


def aligned(value, unit):
    return pl.multiple_of(value * unit, unit)


def off_place(tile, y_tiles, z_tiles):
    a = tile // (y_tiles * z_tiles)
    b = (tile // z_tiles) % y_tiles
    c = tile % z_tiles
    return aligned(a, TW), aligned(b, TW), aligned(c, TL)


def interp_kernel(count, slots, dims, refs):
    (fin, fout, slot_ref, off_ref, near_ref, maps_in, maps_out) = refs[:7]
    outs = refs[7 : 7 + count]
    near_buf, off_buf, in_buf, out_buf, sems = refs[7 + count :]
    rows_here, per_slot, y_tiles, z_tiles = dims
    me = lax.axis_index("gy")
    copies, heads = [], []
    for j in range(count):
        dest = lax.rem(me + j, count)
        k_in, k_out = jnp.int32(0), jnp.int32(0)
        t_in, t_out = jnp.int32(-1), jnp.int32(-1)
        for k in range(rows_here):
            hit = fin[1, k] == dest
            k_in = jnp.where(hit, k, k_in)
            t_in = jnp.where(hit, fin[2, k], t_in)
            hit = fout[1, k] == dest
            k_out = jnp.where(hit, k, k_out)
            t_out = jnp.where(hit, fout[2, k], t_out)
        heads.append((t_in, t_out))
        donor = fin[0, k_in]
        slot, q = donor // per_slot, aligned(donor % per_slot, TW)
        x0, y0, z0 = off_place(fout[0, k_out], y_tiles, z_tiles)
        group = [
            pltpu.make_async_copy(
                near_ref.at[slot, :, :, pl.ds(q, TW), :], near_buf.at[j], sems.at[0, j]
            ),
            pltpu.make_async_copy(maps_in.at[k_in], in_buf.at[j], sems.at[1, j]),
            pltpu.make_async_copy(
                off_ref.at[:, pl.ds(x0, TW), pl.ds(y0, TW), pl.ds(z0, TL)],
                off_buf.at[j],
                sems.at[2, j],
            ),
            pltpu.make_async_copy(maps_out.at[k_out], out_buf.at[j], sems.at[3, j]),
        ]
        for copy in group:
            copy.start()
        copies.append(group)
    lines = FIELDS * TW * TW
    row = lax.broadcasted_iota(jnp.int32, (META, TL), 0)
    for j in range(count):
        for copy in copies[j]:
            copy.wait()
        for side, (tiles, maps) in enumerate(((near_buf, in_buf), (off_buf, out_buf))):
            donors = tiles[j].reshape(lines, TL).astype(jnp.bfloat16)
            mixed = jnp.dot(donors, maps[j], preferred_element_type=jnp.float32)
            outs[j][side * lines : (side + 1) * lines, :] = mixed.astype(jnp.bfloat16)
        head = jnp.where(row == 0, heads[j][0], jnp.where(row == 1, heads[j][1], 0))
        for s in range(slots):
            head = jnp.where(row == 2 + s, slot_ref[s], head)
        outs[j][2 * lines :, :] = head.astype(jnp.float32).astype(jnp.bfloat16)


def base_kernel(slots, dims, refs):
    off_ref, near_ref, metric_ref, layers, faces, edge, medge, sems = refs
    around, nx, ny, nz = dims
    loads = []
    for end, start in enumerate((0, around - TW)):
        for k, (source, target) in enumerate(((near_ref, edge), (metric_ref, medge))):
            loads.append(
                pltpu.make_async_copy(
                    source.at[:, :, :, pl.ds(start, TW), :], target.at[end], sems.at[k, end]
                )
            )
    for copy in loads:
        copy.start()

    def turn(x, _):
        for end, start in enumerate((0, ny - DEPTH)):
            for c in range(FIELDS):
                for d in range(DEPTH):
                    for h in range(nz // TL):
                        layers[end, c * DEPTH + d, h, pl.ds(x, 1), :] = (
                            off_ref[c, x, start + d : start + d + 1, h * TL : (h + 1) * TL]
                            - CENTRE[c]
                        )
        return 0

    lax.fori_loop(0, nx, turn, 0)
    layers[:, FIELDS * DEPTH :] = jnp.ones((2, DEPTH) + layers.shape[2:], jnp.float32)
    for copy in loads:
        copy.wait()
    for s in range(slots):
        for end in range(2):
            number = 0
            for c in range(FIELDS):
                for d in range(DEPTH):
                    layer = d + (0 if end == 0 else TW - DEPTH)
                    slab = face_slab(edge, (end, s, c), layer) - CENTRE[c]
                    faces[s * 2 + end, number * TW : (number + 1) * TW, :] = slab
                    number += 1
            for a in range(3):
                for d in range(DEPTH - 1):
                    layer = d + (0 if end == 0 else TW - DEPTH + 1)
                    slab = face_slab(medge, (end, s, a), layer)
                    faces[s * 2 + end, number * TW : (number + 1) * TW, :] = slab
                    number += 1
            faces[s * 2 + end, number * TW : (number + 1) * TW, :] = jnp.ones(
                (TW, TL), jnp.float32
            )


def patch_kernel(count, dims, refs):
    parcels = refs[:count]
    base_layers, y_low, y_high, table = refs[count : count + 4]
    layers, tiles, wide, head_v, head_s, sems = refs[count + 4 :]
    nx, ny, nz = dims
    y_tiles, z_tiles = ny // TW, nz // TL
    lines = FIELDS * TW * TW
    heads = [
        pltpu.make_async_copy(
            parcels[j].at[pl.ds(2 * lines, META), :],
            tiles.at[j, pl.ds(lines, META), :],
            sems.at[j],
        )
        for j in range(count)
    ]
    bodies = [
        pltpu.make_async_copy(
            parcels[j].at[pl.ds(0, lines), :],
            tiles.at[j, pl.ds(0, lines), :],
            sems.at[count + j],
        )
        for j in range(count)
    ]
    load = pltpu.make_async_copy(base_layers, layers, sems.at[2 * count])
    for copy in heads + bodies + [load]:
        copy.start()
    for j in range(count):
        heads[j].wait()
        head = tiles[j, lines:, :].astype(jnp.float32)
        head_v[j * META : (j + 1) * META, :] = head.astype(jnp.int32)
    head_copy = pltpu.make_async_copy(head_v, head_s, sems.at[2 * count + 1])
    head_copy.start()
    for j in range(count):
        bodies[j].wait()
        wide[j] = tiles[j, :lines, :].astype(jnp.float32)
    load.wait()
    head_copy.wait()
    for j in range(count):
        for r in range(RING):
            table[j * RING + r] = head_s[j * META + r, 0]
    for j in range(count):
        tile = head_s[j * META, 0]
        a = tile // (y_tiles * z_tiles)
        b = (tile // z_tiles) % y_tiles
        h = tile % z_tiles
        x0 = aligned(a, TW)
        for end, edge_tile in enumerate((0, y_tiles - 1)):

            @pl.when((tile >= 0) & (b == edge_tile))
            def _():
                first = 0 if end == 0 else TW - DEPTH
                for c in range(FIELDS):
                    for d in range(DEPTH):
                        slab = wide[j, pl.ds(c * TW * TW + first + d, TW, stride=TW), :]
                        layers[end, c * DEPTH + d, h, pl.ds(x0, TW), :] = slab - CENTRE[c]
                for d in range(DEPTH):
                    layers[end, FIELDS * DEPTH + d, h, pl.ds(x0, TW), :] = jnp.zeros(
                        (TW, TL), jnp.float32
                    )

    for end, out in enumerate((y_low, y_high)):
        out[...] = layers[end].astype(jnp.bfloat16)


def face_slab(ref, lead, layer):
    row = lax.broadcasted_iota(jnp.int32, (TW, TL), 0)
    slab = None
    for i in range(TW):
        line = jnp.broadcast_to(ref[lead + (i, slice(layer, layer + 1), slice(None))], (TW, TL))
        slab = line if slab is None else jnp.where(row == i, line, slab)
    return slab


def fill_kernel(count, per_slot, dims, refs):
    table = refs[0]
    parcels = refs[1 : 1 + count]
    off_ref, base_faces, placed, faces = refs[1 + count : 5 + count]
    tiles, wide, front, sems = refs[5 + count :]
    nx, ny, nz = dims
    y_tiles, z_tiles = ny // TW, nz // TL
    lines = FIELDS * TW * TW
    loads = [pltpu.make_async_copy(parcels[j], tiles.at[j], sems.at[j]) for j in range(count)]
    loads.append(pltpu.make_async_copy(base_faces, front, sems.at[count]))
    for copy in loads:
        copy.start()
    for h in range(z_tiles):
        placed[0:FIELDS, :, h] = off_ref[:, :, :, h * TL : (h + 1) * TL]
    placed[FIELDS] = jnp.full(placed.shape[1:], TIME_STEP, jnp.float32)
    for copy in loads:
        copy.wait()
    for j in range(count):
        tile = table[j * RING + 1]
        s = tile // per_slot
        for end, edge_tile in enumerate((0, per_slot - 1)):

            @pl.when((tile >= 0) & (tile % per_slot == edge_tile))
            def _():
                wide[...] = tiles[j, lines : 2 * lines, :].astype(jnp.float32)
                first = 0 if end == 0 else TW - DEPTH
                for c in range(FIELDS):
                    for d in range(DEPTH):
                        slab = wide[pl.ds(c * TW * TW + first + d, TW, stride=TW), :]
                        number = c * DEPTH + d
                        front[s * 2 + end, number * TW : (number + 1) * TW, :] = slab - CENTRE[c]
                front[s * 2 + end, FACE_ROWS - TW :, :] = jnp.zeros((TW, TL), jnp.float32)

    faces[...] = front[...].astype(jnp.bfloat16)
    for j in range(count):
        tile = table[j * RING]

        @pl.when(tile >= 0)
        def _():
            x0 = (tile // (y_tiles * z_tiles)) * TW
            y0 = aligned((tile // z_tiles) % y_tiles, TW)
            h = tile % z_tiles
            for c in range(FIELDS):
                for i in range(0, TW, 2):
                    start = (c * TW + i) * TW
                    pair = tiles[j, start : start + 2 * TW, :].astype(jnp.float32)
                    for k in range(2):
                        placed[c, x0 + i + k, h, pl.ds(y0, TW), :] = pair[k * TW : (k + 1) * TW]
            for i in range(TW):
                placed[FIELDS, x0 + i, h, pl.ds(y0, TW), :] = jnp.zeros((TW, TL), jnp.float32)


def ghost_rows(low, high, c, h, x, scale):
    row = lax.broadcasted_iota(jnp.int32, (RING, TL), 0)
    tile = jnp.full((RING, TL), QUIET_STATE[c] if c < FIELDS else 1.0, jnp.float32)
    for d in range(DEPTH):
        line = high[c * DEPTH + d, h, pl.ds(x, 1), :] + CENTRE[c]
        tile = jnp.where(row == d, jnp.broadcast_to(line, (RING, TL)), tile)
        line = low[c * DEPTH + d, h, pl.ds(x, 1), :] + CENTRE[c]
        tile = jnp.where(row == RING - DEPTH + d, jnp.broadcast_to(line, (RING, TL)), tile)
    return tile * scale if c == FIELDS else tile


def slab_kernel(dims, refs):
    placed, from_low, from_high, _, x_low, x_high, layers, wide, edge, sems = refs
    nx, ny, nz = dims
    halves = nz // TL
    starts = (0, nx - DEPTH)
    loads = [
        pltpu.make_async_copy(placed.at[:, pl.ds(start, DEPTH)], edge.at[end], sems.at[end])
        for end, start in enumerate(starts)
    ]
    loads += [
        pltpu.make_async_copy(source, layers.at[k], sems.at[2 + k])
        for k, source in enumerate((from_low, from_high))
    ]
    for copy in loads:
        copy.start()
    for copy in loads:
        copy.wait()
    wide[...] = layers[...].astype(jnp.float32)
    low, high = wide.at[0], wide.at[1]
    size = halves * (ny + RING)
    for end, (out, start) in enumerate(((x_low, 0), (x_high, nx - DEPTH))):
        for c in range(FIELDS + 1):
            for d in range(DEPTH):
                parts = []
                for h in range(halves):
                    parts.append(edge[end, c, d, h])
                    parts.append(ghost_rows(low, high, c, h, start + d, TIME_STEP))
                block = jnp.concatenate(parts, axis=0) - CENTRE[c]
                number = c * DEPTH + d
                out[number * size : (number + 1) * size, :] = block.astype(jnp.bfloat16)


def primitives(u):
    density, m0, m1, m2, energy = u
    scaled = VISCOSITY / density
    f = [m0 * scaled, m1 * scaled, m2 * scaled]
    ratio = 0.5 / VISCOSITY
    n0, n1, n2 = ratio * m0, ratio * m1, ratio * m2
    d0, d1, d2 = n0 * f[0], n1 * f[1], n2 * f[2]
    c01, c02, c12 = n0 * f[1], n0 * f[2], n1 * f[2]
    kinetic = (d0 + d1) + d2
    hp = (0.5 * (HEAT_RATIO - 1.0)) * (energy - kinetic)
    f.append(scaled * (kinetic + (2.0 * CONDUCTION / VISCOSITY) * hp))
    enthalpy = ratio * energy + (1.0 / VISCOSITY) * hp
    flux = (
        (0.5 * m0, d0 + hp, c01, c02, enthalpy * f[0]),
        (0.5 * m1, c01, d1 + hp, c12, enthalpy * f[1]),
        (0.5 * m2, c02, c12, d2 + hp, enthalpy * f[2]),
    )
    return f, flux


def off_kernel(dims, refs):
    placed, from_low, from_high, from_left, from_right = refs[:5]
    out, token = refs[5:7]
    layers, slabs, wide, begin, state_one, state_two, sems = refs[7:14]
    flux_x, flux_y, f_s = refs[14:18], refs[18:22], refs[22:26]
    up_z, down_z = refs[26:30], refs[30:34]
    nx, ny, nz = dims
    halves = nz // TL
    rows = ny + RING
    main = FRONT + DEPTH
    load = pltpu.make_async_copy(
        placed, begin.at[:, pl.ds(main, nx), :, pl.ds(0, ny), :], sems.at[0]
    )
    load.start()
    low, high = wide.at[0], wide.at[1]
    received = [
        pltpu.make_async_copy(source, target, sems.at[1 + k])
        for k, (source, target) in enumerate(
            (
                (from_low, layers.at[0]),
                (from_high, layers.at[1]),
                (from_left, slabs.at[0]),
                (from_right, slabs.at[1]),
            )
        )
    ]
    for copy in received:
        copy.start()
    token[...] = jnp.zeros(token.shape, jnp.float32)
    lane = lax.broadcasted_iota(jnp.int32, (TW, TL), 1)
    first_lane, last_lane = lane == 0, lane == TL - 1

    def around_z(parts, distance, mask):
        rolled = [pltpu.roll(part, distance % TL, 1) for part in parts]
        return [jnp.where(mask, rolled[(h - distance) % halves], rolled[h]) for h in range(halves)]

    for copy in received:
        copy.wait()
    wide[...] = layers[...].astype(jnp.float32)
    size = halves * rows
    for side, base in ((slabs.at[0], main - DEPTH), (slabs.at[1], main + nx)):
        for c in range(FIELDS + 1):
            for d in range(DEPTH):
                number = c * DEPTH + d
                block = side[number * size : (number + 1) * size, :].astype(jnp.float32)
                for h in range(halves):
                    begin[c, base + d, h] = block[h * rows : (h + 1) * rows] + CENTRE[c]

    def fill(x, _):
        for c in range(FIELDS + 1):
            for h in range(halves):
                begin[c, x + main, h, ny:rows, :] = ghost_rows(low, high, c, h, x, TIME_STEP)
        return 0

    lax.fori_loop(0, nx, fill, 0)
    load.wait()

    for section, (alpha, beta) in enumerate(SECTIONS):
        last = section == len(SECTIONS) - 1
        source, target = ((begin, state_one), (state_one, state_two), (state_two, out))[section]
        tiles = (ny if last else rows) // TW

        def step(i, turn):
            now, one, two, three = (turn % RINGS, *((turn - k) % RINGS for k in (1, 2, 3)))
            x = i - LAG
            for q in range(rows // TW):
                at = slice(q * TW, (q + 1) * TW)
                base = TW + q * TW
                here, after, before = (slice(base + k, base + k + TW) for k in (0, 1, -1))
                if q < tiles:
                    along_z = []
                    for b in range(FIELDS):
                        up = [up_z[two][b, h, at, :] for h in range(halves)]
                        down = [down_z[two][b, h, at, :] for h in range(halves)]
                        up = around_z(up, -1, last_lane)
                        down = around_z(down, 1, first_lane)
                        along_z.append([up[h] + down[h] for h in range(halves)])
                for h in range(halves):
                    for b in range(FIELDS):
                        if q >= tiles:
                            break
                        k = b - 1
                        rate = along_z[b][h] + (
                            (flux_x[three][b, h, at, :] - flux_x[one][b, h, at, :])
                            + (flux_y[two][b, h, before, :] - flux_y[two][b, h, after, :])
                        )
                        if b > 0:
                            sum_x = f_s[three][k, h, here, :] + f_s[one][k, h, here, :]
                            sum_y = f_s[two][k, h, before, :] + f_s[two][k, h, after, :]
                            rate = rate + ((sum_x + sum_y) - 6.0 * f_s[two][k, h, here, :])
                        moved = source[b, x, h, at, :] + begin[FIELDS, x, h, at, :] * rate
                        if section > 0:
                            moved = alpha * begin[b, x, h, at, :] + beta * moved
                        if last:
                            place = jnp.maximum(x - main, 0)
                            out[b, place, at, h * TL : (h + 1) * TL] = moved
                        else:
                            target[b, x, h, at, :] = moved
                    f, flux = primitives([source[c, i, h, at, :] for c in range(FIELDS)])
                    wrap = None
                    if q == 0:
                        wrap = slice(TW + rows, 2 * TW + rows)
                    if (q + 1) * TW == rows:
                        wrap = slice(0, TW)
                    for b in range(FIELDS):
                        if q < tiles:
                            flux_x[now][b, h, at, :] = flux[0][b]
                        flux_y[now][b, h, here, :] = flux[1][b]
                        if wrap is not None:
                            flux_y[now][b, h, wrap, :] = flux[1][b]
                        if b > 0:
                            f_s[now][b - 1, h, here, :] = f[b - 1]
                            if wrap is not None:
                                f_s[now][b - 1, h, wrap, :] = f[b - 1]
                    if q < tiles:
                        for b in range(FIELDS):
                            part = flux[2][b]
                            up_z[now][b, h, at, :] = f[b - 1] - part if b > 0 else -part
                            down_z[now][b, h, at, :] = f[b - 1] + part if b > 0 else part

        reach = DEPTH - 1 - section
        stop = main + nx + reach + LAG
        turns = -(-(nx + 2 * reach + LAG + 1) // RINGS)

        def body(j, _):
            for turn in range(RINGS):
                step(stop - turns * RINGS + j * RINGS + turn, turn)
            return 0

        lax.fori_loop(0, turns, body, 0)


def find(table, count, slots, block):
    where_j, where_t = jnp.int32(0), jnp.int32(0)
    for j in range(count):
        for t in range(slots):
            hit = table[j * RING + 2 + t] == block
            where_j = jnp.where(hit, j, where_j)
            where_t = jnp.where(hit, t, where_t)
    return where_j, where_t


def pack_kernel(count, slots, refs):
    table, block_faces = refs[:2]
    held = refs[2 : 2 + count // 2]
    packed, sems = refs[4 + count // 2 :]
    me = lax.axis_index("gy")
    offset = jnp.where(lax.rem(me, 2) == 1, 1, count - 1)
    for phase in range(2):
        for s in range(slots):
            block = table[offset * RING + 2 + s]

            @pl.when(block >= 0)
            def _():
                for side in range(2):
                    j, t = find(table, count, slots, block_faces[block, side])
                    for m in range(count // 2):

                        @pl.when(j == 2 * m)
                        def _():
                            number = s * 2 + side
                            copy = pltpu.make_async_copy(
                                held[m].at[t * 2 + 1 - side], packed.at[number], sems.at[number]
                            )
                            if phase == 0:
                                copy.start()
                            else:
                                copy.wait()


def near_kernel(count, slots, dims, edges, refs):
    per_slot, around, normal = dims
    table, block_faces, slot_ref, near_ref, metric_ref = refs[:5]
    parcels = refs[5 : 5 + count]
    refs = refs[5 + count :]
    if edges:
        held, packed, main_ref = refs[: count // 2], refs[count // 2], refs[count // 2 + 1]
        out_ref = refs[count // 2 + 3]
        scratch = refs[count // 2 + 4 :]
        own = 2 * TW
        rows = own + RING
    else:
        out_ref, token = refs[1:3]
        scratch = refs[3:]
        token[...] = jnp.zeros(token.shape, jnp.float32)
        own = rows = around
    begins, metrics, state_one, state_two, square, coeff, hold, out, along = scratch[:9]
    tile_buf, in_sems, out_sems, tile_sems = scratch[9:13]
    rings = scratch[13:37]
    flux_n, flux_a, f_s = rings[:4], rings[4:8], rings[8:12]
    up_s, down_s, own_s = rings[12:16], rings[16:20], rings[20:24]
    if edges:
        ghost, face_buf, main_buf, face_sems, main_sems = scratch[37:]
    lines = FIELDS * TW * TW
    wall = (-1.0, 1.0, 1.0, 1.0, -1.0)
    mirror = (-1.0, -1.0, -1.0, 1.0)
    pieces = ((0, 0), (around - TW, TW)) if edges else ((0, 0),)
    piece = TW if edges else around

    def loads(s):
        side = lax.rem(s, 2)
        return [
            pltpu.make_async_copy(
                ref.at[s, :, :, pl.ds(source, piece), :],
                buf.at[side, :, :, pl.ds(target, piece), :],
                in_sems.at[k, p, side],
            )
            for k, (ref, buf) in enumerate(((near_ref, begins), (metric_ref, metrics)))
            for p, (source, target) in enumerate(pieces)
        ]

    def main_loads(s):
        return [
            pltpu.make_async_copy(
                main_ref.at[s, :, :, pl.ds(source, TW), :],
                main_buf.at[s, :, :, pl.ds(target, TW), :],
                main_sems.at[s, p],
            )
            for p, (source, target) in enumerate(pieces)
        ]

    def stores(s):
        return [
            pltpu.make_async_copy(
                out.at[s, :, :, pl.ds(target, piece), :],
                out_ref.at[s, :, :, pl.ds(source, piece), :],
                out_sems.at[s, p],
            )
            for p, (source, target) in enumerate(pieces)
        ]

    def start_loads(s):
        @pl.when(slot_ref[s] >= 0)
        def _():
            for copy in loads(s):
                copy.start()

    start_loads(0)
    lane = lax.broadcasted_iota(jnp.int32, (rows, TL), 1)
    tile_loads = [
        pltpu.make_async_copy(
            parcels[j].at[pl.ds(lines, lines), :], tile_buf.at[j], tile_sems.at[j]
        )
        for j in range(count)
    ]
    for copy in tile_loads:
        copy.start()

    def face_loads(s):
        for side in range(2):
            j, t = find(table, count, slots, block_faces[slot_ref[s], side])
            target, sem = face_buf.at[s, side], face_sems.at[s, side]
            for m in range(count // 2):

                @pl.when(j == 2 * m)
                def _():
                    pltpu.make_async_copy(held[m].at[t * 2 + 1 - side], target, sem).start()

            @pl.when(lax.rem(j, 2) == 1)
            def _():
                pltpu.make_async_copy(packed.at[s * 2 + side], target, sem).start()

    if edges:
        for s in range(slots):

            @pl.when(slot_ref[s] >= 0)
            def _():
                face_loads(s)
                for copy in main_loads(s):
                    copy.start()

    for copy in tile_loads:
        copy.wait()
    row = lax.broadcasted_iota(jnp.int32, (RING, TL), 0)

    def take_ghosts(s, begin, metric):
        for side in range(2):
            pltpu.make_async_copy(
                packed.at[0], face_buf.at[s, side], face_sems.at[s, side]
            ).wait()
            ghost[side] = face_buf[s, side].astype(jnp.float32)

        def ghost_tile(number, layers, i, fill, centre):
            tile = jnp.full((RING, TL), fill, jnp.float32)
            for d in range(layers):
                at = (number + d) * TW + i
                line = jnp.broadcast_to(ghost[1, at : at + 1, :] + centre, (RING, TL))
                tile = jnp.where(row == d, line, tile)
                line = jnp.broadcast_to(ghost[0, at : at + 1, :] + centre, (RING, TL))
                tile = jnp.where(row == RING - layers + d, line, tile)
            return tile

        step = DEPTH - 1
        for i in range(normal):
            for c in range(FIELDS):
                begin[c, i, own:rows, :] = ghost_tile(
                    c * DEPTH, DEPTH, i, QUIET_STATE[c], CENTRE[c]
                )
            for a in range(3):
                metric[a, i, own:rows, :] = ghost_tile(
                    FIELDS * DEPTH + a * step, step, i, 1.0, 0.0
                )
        last_layer = (FACE_LAYERS - 1) * TW
        hold[own:rows, :] = TIME_STEP * jnp.where(
            row < RING // 2,
            ghost[1, last_layer : last_layer + TW, :],
            ghost[0, last_layer : last_layer + TW, :],
        )

    def slot_work(s, _):
        begin, metric = begins.at[lax.rem(s, 2)], metrics.at[lax.rem(s, 2)]

        @pl.when(s + 1 < slots)
        def _():
            start_loads(jnp.minimum(s + 1, slots - 1))

        if not edges:

            @pl.when(slot_ref[s] < 0)
            def _():
                out[s] = jnp.zeros(out.shape[1:], jnp.float32)

        @pl.when(slot_ref[s] >= 0)
        def _():
            if edges:
                take_ghosts(s, begin, metric)
            hold[0:own, :] = jnp.full((own, TL), TIME_STEP, jnp.float32)
            for copy in loads(s):
                copy.wait()
            if edges:
                for copy in main_loads(s):
                    copy.wait()
            for j in range(count):
                tile = table[j * RING + 1]
                number = tile % per_slot
                mine = (tile >= 0) & (tile // per_slot == s)
                if edges:
                    mine = mine & ((number == 0) | (number == per_slot - 1))
                    number = jnp.where(number == 0, 0, 1)

                @pl.when(mine)
                def _():
                    q = aligned(number, TW)
                    for c in range(FIELDS):
                        for i in range(0, TW, 2):
                            start = (c * TW + i) * TW
                            pair = tile_buf[j, start : start + 2 * TW, :].astype(jnp.float32)
                            begin[c, i, pl.ds(q, TW), :] = pair[:TW]
                            begin[c, i + 1, pl.ds(q, TW), :] = pair[TW:]
                    hold[pl.ds(q, TW), :] = jnp.zeros((TW, TL), jnp.float32)

            def prepare(i, _):
                squares = [metric[a, i] * metric[a, i] for a in range(3)]
                for a in range(2):
                    square[a, i] = squares[a]
                total = -2.0 * ((squares[0] + squares[1]) + squares[2])
                at_end = (lane == 0) | (lane == TL - 1)
                coeff[i] = jnp.where(at_end, total + squares[2], total)
                g = metric[2, i]
                along[0, i] = jnp.where(lane == 0, 0.0, pltpu.roll(g, 1, 1))
                along[1, i] = jnp.where(lane == TL - 1, 0.0, pltpu.roll(g, TL - 1, 1))
                along[2, i] = jnp.where(lane == 0, g, jnp.where(lane == TL - 1, -g, 0.0))
                return 0

            lax.fori_loop(0, normal, prepare, 0)

            for section, (alpha, beta) in enumerate(SECTIONS):
                last = section == len(SECTIONS) - 1
                source = (begin, state_one, state_two)[section]
                target = (state_one, state_two, out)[section]
                tiles = (own if last else rows) // TW

                def advance(x, q):
                    at = slice(q * TW, (q + 1) * TW)
                    base = TW + q * TW
                    here, after, before = (slice(base + k, base + k + TW) for k in (0, 1, -1))
                    mid, low = x % RINGS, (x - 1) % RINGS
                    high = (x + 1) % RINGS
                    g = [metric[a, x, at, :] for a in range(2)]
                    g2 = [square[a, x, at, :] for a in range(2)]
                    center = coeff[x, at, :]
                    for b in range(FIELDS):
                        k = b - 1
                        rate = pltpu.roll(up_s[mid][b, at, :], TL - 1, 1)
                        rate = rate + pltpu.roll(down_s[mid][b, at, :], 1, 1)
                        rate = rate + own_s[mid][b, at, :]
                        rate = rate + g[0] * (flux_n[low][b, at, :] - flux_n[high][b, at, :])
                        rate = rate + g[1] * (
                            flux_a[mid][b, before, :] - flux_a[mid][b, after, :]
                        )
                        if b > 0:
                            rate = rate + g2[0] * (f_s[low][k, here, :] + f_s[high][k, here, :])
                            rate = rate + g2[1] * (
                                f_s[mid][k, before, :] + f_s[mid][k, after, :]
                            )
                            rate = rate + center * f_s[mid][k, here, :]
                        moved = source[b, x, at, :] + hold[at, :] * rate
                        if section > 0:
                            moved = alpha * begin[b, x, at, :] + beta * moved
                        if last and edges:
                            right = row < DEPTH if q == 0 else row >= TW - DEPTH
                            moved = jnp.where(right, moved, main_buf[s, b, x, at, :])
                        if last:
                            out[s, b, x, at, :] = moved
                        else:
                            target[b, x, at, :] = moved

                def work(i, q):
                    at = slice(q * TW, (q + 1) * TW)
                    base = TW + q * TW
                    here = slice(base, base + TW)
                    now = i % RINGS
                    f, flux = primitives([source[c, i, at, :] for c in range(FIELDS)])
                    wrap = None
                    if q == 0:
                        wrap = slice(TW + rows, 2 * TW + rows)
                    if base == rows:
                        wrap = slice(0, TW)
                    for b in range(FIELDS):
                        if q < tiles:
                            flux_n[now][b, at, :] = flux[0][b]
                            if i == 0:
                                flux_n[now - 1][b, at, :] = wall[b] * flux[0][b]
                            if i == normal - 1:
                                flux_n[(now + 1) % RINGS][b, at, :] = flux[0][b]
                        flux_a[now][b, here, :] = flux[1][b]
                        if wrap is not None:
                            flux_a[now][b, wrap, :] = flux[1][b]
                        if b > 0:
                            f_s[now][b - 1, here, :] = f[b - 1]
                            if wrap is not None:
                                f_s[now][b - 1, wrap, :] = f[b - 1]
                            if i == 0:
                                f_s[now - 1][b - 1, here, :] = mirror[b - 1] * f[b - 1]
                            if i == normal - 1:
                                f_s[(now + 1) % RINGS][b - 1, here, :] = f[b - 1]
                    if q < tiles:
                        g_up, g_down = along[0, i, at, :], along[1, i, at, :]
                        g_own = along[2, i, at, :]
                        for b in range(FIELDS):
                            part = flux[2][b]
                            if b > 0:
                                up_s[now][b, at, :] = g_up * (g_up * f[b - 1] - part)
                                down_s[now][b, at, :] = g_down * (g_down * f[b - 1] + part)
                            else:
                                up_s[now][b, at, :] = -(g_up * part)
                                down_s[now][b, at, :] = g_down * part
                            own_s[now][b, at, :] = g_own * part

                for i in range(normal + LAG):
                    for q in range(rows // TW):
                        if i >= LAG and q < tiles:
                            advance(i - LAG, q)
                        if i < normal:
                            work(i, q)

        def send_out():
            for copy in stores(s):
                copy.start()

        if edges:
            pl.when(slot_ref[s] >= 0)(send_out)
        else:
            send_out()
        return 0

    lax.fori_loop(0, slots, slot_work, 0)
    for s in range(slots):

        def end_out():
            for copy in stores(s):
                copy.wait()

        if edges:
            pl.when(slot_ref[s] >= 0)(end_out)
        else:
            end_out()


def packed_refs(kernel, *first):
    def body(*refs):
        kernel(*first, refs)

    return body


def off_call(placed, from_low, from_high, from_left, from_right):
    _, nx, halves, ny, _ = placed.shape
    nz = halves * TL
    f32, shape = jnp.float32, jax.ShapeDtypeStruct
    rows = ny + RING
    slices = FRONT + nx + 2 * DEPTH + 2
    return pl.pallas_call(
        packed_refs(off_kernel, (nx, ny, nz)),
        out_shape=[shape((FIELDS, nx, ny, nz), f32), shape((RING, TL), f32)],
        in_specs=[any_spec()] * 5,
        out_specs=[vmem_spec()] * 2,
        scratch_shapes=[
            VMEM((2,) + from_low.shape, jnp.bfloat16),
            VMEM((2,) + from_left.shape, jnp.bfloat16),
            VMEM((2,) + from_low.shape, f32),
            VMEM((FIELDS + 1, slices, halves, rows, TL), f32),
            VMEM((FIELDS, slices, halves, rows, TL), f32),
            VMEM((FIELDS, slices, halves, rows, TL), f32),
            pltpu.SemaphoreType.DMA((5,)),
        ]
        + [VMEM((FIELDS, halves, rows, TL), f32)] * RINGS
        + [VMEM((FIELDS, halves, rows + 2 * TW, TL), f32)] * RINGS
        + [VMEM((FIELDS - 1, halves, rows + 2 * TW, TL), f32)] * RINGS
        + [VMEM((FIELDS, halves, rows, TL), f32)] * RINGS * 2,
        compiler_params=params(40),
        cost_estimate=cost(1e8, 5e7),
        name="off_sections",
    )(placed, from_low, from_high, from_left, from_right)


def near_call(table, block_faces, slot_block, near_state, near_metric, parcels, edges, after):
    count = len(parcels)
    slots, _, normal, around, _ = near_state.shape
    f32, shape = jnp.float32, jax.ShapeDtypeStruct
    dma = pltpu.SemaphoreType.DMA
    own = 2 * TW if edges else around
    rows = own + RING if edges else own
    pieces = 2 if edges else 1
    out_shape = [shape(near_state.shape, f32)]
    out_specs = [any_spec()]
    extra, aliases = [], {}
    if edges:
        aliases = {5 + count + count // 2 + 1: 0}
        extra = [
            VMEM((2, FACE_ROWS, TL), f32),
            VMEM((slots, 2, FACE_ROWS, TL), jnp.bfloat16),
            VMEM((slots, FIELDS, normal, own, TL), f32),
            dma((slots, 2)),
            dma((slots, 2)),
        ]
    else:
        out_shape.append(shape((RING, TL), f32))
        out_specs.append(vmem_spec())
    return pl.pallas_call(
        packed_refs(near_kernel, count, slots, (around // TW, around, normal), edges),
        out_shape=out_shape,
        in_specs=[smem_spec()] * 3 + [any_spec()] * (2 + count + len(after)),
        out_specs=out_specs,
        input_output_aliases=aliases,
        scratch_shapes=[
            VMEM((2, FIELDS, normal, rows, TL), f32),
            VMEM((2, 3, normal, rows, TL), f32),
            VMEM((FIELDS, normal, rows, TL), f32),
            VMEM((FIELDS, normal, rows, TL), f32),
            VMEM((2, normal, rows, TL), f32),
            VMEM((normal, rows, TL), f32),
            VMEM((rows, TL), f32),
            VMEM((slots, FIELDS, normal, own, TL), f32),
            VMEM((3, normal, rows, TL), f32),
            VMEM((count, FIELDS * TW * TW, TL), jnp.bfloat16),
            dma((2, pieces, 2)),
            dma((slots, pieces)),
            dma((count,)),
        ]
        + [VMEM((FIELDS, rows, TL), f32)] * RINGS
        + [VMEM((FIELDS, rows + 2 * TW, TL), f32)] * RINGS
        + [VMEM((FIELDS - 1, rows + 2 * TW, TL), f32)] * RINGS
        + [VMEM((FIELDS, rows, TL), f32)] * RINGS * 3
        + extra,
        compiler_params=params(VMEM_MIB),
        cost_estimate=cost(1e8, 5e7),
        name="near_edges" if edges else "near_sections",
    )(table, block_faces, slot_block, near_state, near_metric, *parcels, *after)


def ring(axis, distance):
    count = lax.axis_size(axis)
    return [(i, (i + distance) % count) for i in range(count)]


def send(value, axis, distance):
    return lax.ppermute(value, axis, ring(axis, distance))


def local(
    off_state,
    near_state,
    near_metric,
    slot_block,
    block_faces,
    fringe_in,
    fringe_in_maps,
    fringe_out,
    fringe_out_maps,
):
    count = lax.axis_size("gy")
    slots, _, normal, around, span = near_state.shape
    _, nx, ny, nz = off_state.shape
    rows_here = fringe_in.shape[1]
    per_slot = around // TW
    lines = FIELDS * TW * TW
    half, f32 = jnp.bfloat16, jnp.float32
    shape = jax.ShapeDtypeStruct
    tile_buf = VMEM((count, FIELDS, TW, TW, TL), f32)
    map_buf = VMEM((count, TL, TL), half)

    parcels = pl.pallas_call(
        packed_refs(
            interp_kernel, count, slots, (rows_here, per_slot, ny // TW, nz // TL)
        ),
        out_shape=[shape((2 * lines + META, TL), half)] * count,
        in_specs=[smem_spec()] * 3 + [any_spec()] * 4,
        out_specs=[vmem_spec()] * count,
        scratch_shapes=[
            tile_buf,
            tile_buf,
            map_buf,
            map_buf,
            pltpu.SemaphoreType.DMA((4, count)),
        ],
        compiler_params=params(VMEM_MIB),
        cost_estimate=cost(2e8, 6e6),
        name="interp",
    )(fringe_in, fringe_out, slot_block, off_state, near_state, fringe_in_maps, fringe_out_maps)
    dma = pltpu.SemaphoreType.DMA
    planes = (FIELDS + 1) * DEPTH
    halves = nz // TL
    layer_shape = (planes, halves, nx, TL)
    base_layers, base_faces = pl.pallas_call(
        packed_refs(base_kernel, slots, (around, nx, ny, nz)),
        out_shape=[
            shape((2,) + layer_shape, f32),
            shape((2 * slots, FACE_ROWS, TL), f32),
        ],
        in_specs=[vmem_spec()] + [any_spec()] * 2,
        out_specs=[vmem_spec()] * 2,
        scratch_shapes=[
            VMEM((2, slots, FIELDS, normal, TW, TL), f32),
            VMEM((2, slots, 3, normal, TW, TL), f32),
            dma((2, 2)),
        ],
        compiler_params=params(VMEM_MIB),
        cost_estimate=cost(1e7, 2e7),
        name="base",
    )(off_state, near_state, near_metric)

    parcels = [parcels[0]] + [send(parcels[j], "gy", j) for j in range(1, count)]

    y_low, y_high, table = pl.pallas_call(
        packed_refs(patch_kernel, count, (nx, ny, nz)),
        out_shape=[
            shape(layer_shape, half),
            shape(layer_shape, half),
            shape((count * RING,), jnp.int32),
        ],
        in_specs=[any_spec()] * (count + 1),
        out_specs=[vmem_spec()] * 2 + [smem_spec()],
        scratch_shapes=[
            VMEM((2,) + layer_shape, f32),
            VMEM((count, lines + META, TL), half),
            VMEM((count, lines, TL), f32),
            VMEM((count * META, TL), jnp.int32),
            SMEM((count * META, TL), jnp.int32),
            dma((2 * count + 2,)),
        ],
        compiler_params=params(12),
        cost_estimate=cost(1e7, 8e6),
        name="patch",
    )(*parcels, base_layers)

    from_low = send(y_high, "gy", 1)
    from_high = send(y_low, "gy", count - 1)

    placed, faces = pl.pallas_call(
        packed_refs(fill_kernel, count, per_slot, (nx, ny, nz)),
        out_shape=[
            shape((FIELDS + 1, nx, halves, ny, TL), f32),
            shape((2 * slots, FACE_ROWS, TL), half),
        ],
        in_specs=[smem_spec()] + [any_spec()] * count + [vmem_spec()] + [any_spec()],
        out_specs=[vmem_spec()] * 2,
        scratch_shapes=[
            VMEM((count, 2 * lines + META, TL), half),
            VMEM((lines, TL), f32),
            VMEM((2 * slots, FACE_ROWS, TL), f32),
            dma((count + 1,)),
        ],
        compiler_params=params(VMEM_MIB),
        cost_estimate=cost(1e7, 1e7),
        name="fill",
    )(table, *parcels, off_state, base_faces)
    held = [faces] + [send(faces, "gy", 2 * m) for m in range(1, count // 2)]

    near_main, near_token = near_call(
        table, block_faces, slot_block, near_state, near_metric, parcels, False, [faces]
    )

    x_low, x_high = pl.pallas_call(
        packed_refs(slab_kernel, (nx, ny, nz)),
        out_shape=[shape((planes * halves * (ny + RING), TL), half)] * 2,
        in_specs=[any_spec()] * 4,
        out_specs=[vmem_spec()] * 2,
        scratch_shapes=[
            VMEM((2,) + layer_shape, half),
            VMEM((2,) + layer_shape, f32),
            VMEM((2, FIELDS + 1, DEPTH, halves, ny, TL), f32),
            dma((4,)),
        ],
        compiler_params=params(8),
        cost_estimate=cost(1e6, 4e6),
        name="slabs",
    )(placed, from_low, from_high, near_token)
    from_left = send(x_high, "gx", 1)
    from_right = send(x_low, "gx", lax.axis_size("gx") - 1)

    packed = pl.pallas_call(
        packed_refs(pack_kernel, count, slots),
        out_shape=shape((2 * slots, FACE_ROWS, TL), half),
        in_specs=[smem_spec()] * 2 + [any_spec()] * (count // 2 + 2),
        out_specs=any_spec(),
        scratch_shapes=[dma((2 * slots,))],
        compiler_params=params(4),
        cost_estimate=cost(1e5, 2e6),
        name="pack",
    )(table, block_faces, *held, from_left, from_right)
    packed = lax.ppermute(packed, "gy", [(i, i ^ 1) for i in range(count)])

    off_next, off_token = off_call(placed, from_low, from_high, from_left, from_right)
    after = [*held, packed, near_main, off_token]
    (near_next,) = near_call(
        table, block_faces, slot_block, near_state, near_metric, parcels, True, after
    )
    return off_next, near_next


def solution(mesh):
    in_specs = (
        P(None, "gx", "gy", None),
        P(("gx", "gy"), None, None, None, None),
        P(("gx", "gy"), None, None, None, None),
        P(("gx", "gy")),
        P(),
        P(None, ("gx", "gy")),
        P(("gx", "gy"), None, None),
        P(None, ("gx", "gy")),
        P(("gx", "gy"), None, None),
    )
    out_specs = (P(None, "gx", "gy", None), P(("gx", "gy"), None, None, None, None))
    return jax.shard_map(local, mesh=mesh, in_specs=in_specs, out_specs=out_specs, check_vma=False)
```

```python
import functools

import jax
import jax.numpy as jnp
from jax import lax
from jax.experimental import pallas as pl
from jax.experimental.pallas import tpu as pltpu
from jax.sharding import PartitionSpec as P

TW = 8
TL = 128
DEPTH = 3
RING = 8
META = 16
FIELDS = 5
HEAT_RATIO = 1.4
VISCOSITY = 0.8
CONDUCTION = 1.12
TIME_STEP = 0.1
QUIET_STATE = (1.0, 0.0, 0.0, 0.0, 2.5)
CENTRE = (1.0, 0.0, 0.0, 0.0, 2.5, 0.0)
SECTIONS = ((0.0, 1.0), (0.75, 0.25), (1.0 / 3.0, 2.0 / 3.0))
FACE_LAYERS = FIELDS * DEPTH + 3 * (DEPTH - 1) + 1
FACE_ROWS = FACE_LAYERS * TW
LAG = 2
RINGS = 4
VMEM_MIB = 61
FRONT = 6

VMEM = pltpu.VMEM
SMEM = pltpu.SMEM


def vmem_spec():
    return pl.BlockSpec(memory_space=VMEM)


def smem_spec():
    return pl.BlockSpec(memory_space=SMEM)


def any_spec():
    return pl.BlockSpec(memory_space=pl.ANY)


def params(mebibytes):
    return pltpu.CompilerParams(vmem_limit_bytes=mebibytes * 1024 * 1024)


def cost(flops, moved):
    return pl.CostEstimate(flops=int(flops), bytes_accessed=int(moved), transcendentals=0)


def aligned(value, unit):
    return pl.multiple_of(value * unit, unit)


def off_place(tile, y_tiles, z_tiles):
    a = tile // (y_tiles * z_tiles)
    b = (tile // z_tiles) % y_tiles
    c = tile % z_tiles
    return aligned(a, TW), aligned(b, TW), aligned(c, TL)


def interp_kernel(count, slots, dims, refs):
    (fin, fout, slot_ref, off_ref, near_ref, maps_in, maps_out) = refs[:7]
    outs = refs[7 : 7 + count]
    near_buf, off_buf, in_buf, out_buf, sems = refs[7 + count :]
    rows_here, per_slot, y_tiles, z_tiles = dims
    me = lax.axis_index("gy")
    copies, heads = [], []
    for j in range(count):
        dest = lax.rem(me + j, count)
        k_in, k_out = jnp.int32(0), jnp.int32(0)
        t_in, t_out = jnp.int32(-1), jnp.int32(-1)
        for k in range(rows_here):
            hit = fin[1, k] == dest
            k_in = jnp.where(hit, k, k_in)
            t_in = jnp.where(hit, fin[2, k], t_in)
            hit = fout[1, k] == dest
            k_out = jnp.where(hit, k, k_out)
            t_out = jnp.where(hit, fout[2, k], t_out)
        heads.append((t_in, t_out))
        donor = fin[0, k_in]
        slot, q = donor // per_slot, aligned(donor % per_slot, TW)
        x0, y0, z0 = off_place(fout[0, k_out], y_tiles, z_tiles)
        group = [
            pltpu.make_async_copy(
                near_ref.at[slot, :, :, pl.ds(q, TW), :], near_buf.at[j], sems.at[0, j]
            ),
            pltpu.make_async_copy(maps_in.at[k_in], in_buf.at[j], sems.at[1, j]),
            pltpu.make_async_copy(
                off_ref.at[:, pl.ds(x0, TW), pl.ds(y0, TW), pl.ds(z0, TL)],
                off_buf.at[j],
                sems.at[2, j],
            ),
            pltpu.make_async_copy(maps_out.at[k_out], out_buf.at[j], sems.at[3, j]),
        ]
        for copy in group:
            copy.start()
        copies.append(group)
    lines = FIELDS * TW * TW
    row = lax.broadcasted_iota(jnp.int32, (META, TL), 0)
    for j in range(count):
        for copy in copies[j]:
            copy.wait()
        for side, (tiles, maps) in enumerate(((near_buf, in_buf), (off_buf, out_buf))):
            donors = tiles[j].reshape(lines, TL).astype(jnp.bfloat16)
            mixed = jnp.dot(donors, maps[j], preferred_element_type=jnp.float32)
            outs[j][side * lines : (side + 1) * lines, :] = mixed.astype(jnp.bfloat16)
        head = jnp.where(row == 0, heads[j][0], jnp.where(row == 1, heads[j][1], 0))
        for s in range(slots):
            head = jnp.where(row == 2 + s, slot_ref[s], head)
        outs[j][2 * lines :, :] = head.astype(jnp.float32).astype(jnp.bfloat16)


def base_kernel(slots, dims, refs):
    off_ref, near_ref, metric_ref, layers, faces, placed, edge, medge, sems = refs
    around, nx, ny, nz = dims
    loads = []
    for end, start in enumerate((0, around - TW)):
        for k, (source, target) in enumerate(((near_ref, edge), (metric_ref, medge))):
            loads.append(
                pltpu.make_async_copy(
                    source.at[:, :, :, pl.ds(start, TW), :], target.at[end], sems.at[k, end]
                )
            )
    for copy in loads:
        copy.start()

    for h in range(nz // TL):
        placed[0:FIELDS, :, h] = off_ref[:, :, :, h * TL : (h + 1) * TL]
    placed[FIELDS] = jnp.full(placed.shape[1:], TIME_STEP, jnp.float32)

    def turn(x, _):
        for end, start in enumerate((0, ny - DEPTH)):
            for c in range(FIELDS):
                for d in range(DEPTH):
                    for h in range(nz // TL):
                        layers[end, c * DEPTH + d, h, pl.ds(x, 1), :] = (
                            off_ref[c, x, start + d : start + d + 1, h * TL : (h + 1) * TL]
                            - CENTRE[c]
                        )
        return 0

    lax.fori_loop(0, nx, turn, 0)
    layers[:, FIELDS * DEPTH :] = jnp.ones((2, DEPTH) + layers.shape[2:], jnp.float32)
    for copy in loads:
        copy.wait()
    for s in range(slots):
        for end in range(2):
            number = 0
            for c in range(FIELDS):
                for d in range(DEPTH):
                    layer = d + (0 if end == 0 else TW - DEPTH)
                    slab = face_slab(edge, (end, s, c), layer) - CENTRE[c]
                    faces[s * 2 + end, number * TW : (number + 1) * TW, :] = slab
                    number += 1
            for a in range(3):
                for d in range(DEPTH - 1):
                    layer = d + (0 if end == 0 else TW - DEPTH + 1)
                    slab = face_slab(medge, (end, s, a), layer)
                    faces[s * 2 + end, number * TW : (number + 1) * TW, :] = slab
                    number += 1
            faces[s * 2 + end, number * TW : (number + 1) * TW, :] = jnp.ones(
                (TW, TL), jnp.float32
            )


def patch_kernel(count, per_slot, dims, refs):
    parcels = refs[:count]
    base_layers, base_faces, _, y_low, y_high, faces, table, placed = refs[count : count + 8]
    layers, front, tiles, wide, near_wide, nothing, head_v, head_s, sems, out_sems = refs[count + 8 :]
    nx, ny, nz = dims
    y_tiles, z_tiles = ny // TW, nz // TL
    lines = FIELDS * TW * TW
    heads = [
        pltpu.make_async_copy(
            parcels[j].at[pl.ds(2 * lines, META), :],
            tiles.at[j, pl.ds(2 * lines, META), :],
            sems.at[j],
        )
        for j in range(count)
    ]
    bodies = [
        pltpu.make_async_copy(
            parcels[j].at[pl.ds(0, 2 * lines), :],
            tiles.at[j, pl.ds(0, 2 * lines), :],
            sems.at[count + j],
        )
        for j in range(count)
    ]
    rest = [
        pltpu.make_async_copy(base_layers, layers, sems.at[2 * count]),
        pltpu.make_async_copy(base_faces, front, sems.at[2 * count + 1]),
    ]
    for copy in heads + bodies + rest:
        copy.start()
    nothing[...] = jnp.zeros(nothing.shape, jnp.float32)
    for j in range(count):
        heads[j].wait()
        head = tiles[j, 2 * lines :, :].astype(jnp.float32)
        head_v[j * META : (j + 1) * META, :] = head.astype(jnp.int32)
    head_copy = pltpu.make_async_copy(head_v, head_s, sems.at[2 * count + 2])
    head_copy.start()
    for j in range(count):
        bodies[j].wait()
        wide[j] = tiles[j, :lines, :].astype(jnp.float32)
    for copy in rest:
        copy.wait()
    head_copy.wait()
    for j in range(count):
        for r in range(RING):
            table[j * RING + r] = head_s[j * META + r, 0]

    def tile_place(j):
        tile = head_s[j * META, 0]
        a = tile // (y_tiles * z_tiles)
        b = (tile // z_tiles) % y_tiles
        return tile, aligned(a, TW), b, tile % z_tiles

    def tile_copies(j):
        tile, x0, b, h = tile_place(j)
        at = (pl.ds(x0, TW), h, pl.ds(aligned(b, TW), TW), slice(None))
        return [
            pltpu.make_async_copy(
                wide.at[j].reshape(FIELDS, TW, TW, TL),
                placed.at[(pl.ds(0, FIELDS),) + at],
                out_sems.at[0, j],
            ),
            pltpu.make_async_copy(nothing, placed.at[(FIELDS,) + at], out_sems.at[1, j]),
        ]

    for j in range(count):
        tile, x0, b, h = tile_place(j)

        @pl.when(tile >= 0)
        def _():
            for copy in tile_copies(j):
                copy.start()

        for end, edge_tile in enumerate((0, y_tiles - 1)):

            @pl.when((tile >= 0) & (b == edge_tile))
            def _():
                first = 0 if end == 0 else TW - DEPTH
                for c in range(FIELDS):
                    for d in range(DEPTH):
                        slab = wide[j, pl.ds(c * TW * TW + first + d, TW, stride=TW), :]
                        layers[end, c * DEPTH + d, h, pl.ds(x0, TW), :] = slab - CENTRE[c]
                for d in range(DEPTH):
                    layers[end, FIELDS * DEPTH + d, h, pl.ds(x0, TW), :] = jnp.zeros(
                        (TW, TL), jnp.float32
                    )

        tile = head_s[j * META + 1, 0]
        s = tile // per_slot
        for end, edge_tile in enumerate((0, per_slot - 1)):

            @pl.when((tile >= 0) & (tile % per_slot == edge_tile))
            def _():
                near_wide[...] = tiles[j, lines : 2 * lines, :].astype(jnp.float32)
                first = 0 if end == 0 else TW - DEPTH
                for c in range(FIELDS):
                    for d in range(DEPTH):
                        slab = near_wide[pl.ds(c * TW * TW + first + d, TW, stride=TW), :]
                        number = c * DEPTH + d
                        front[s * 2 + end, number * TW : (number + 1) * TW, :] = slab - CENTRE[c]
                front[s * 2 + end, FACE_ROWS - TW :, :] = jnp.zeros((TW, TL), jnp.float32)

    for end, out in enumerate((y_low, y_high)):
        out[...] = layers[end].astype(jnp.bfloat16)
    faces[...] = front[...].astype(jnp.bfloat16)
    for j in range(count):

        @pl.when(head_s[j * META, 0] >= 0)
        def _():
            for copy in tile_copies(j):
                copy.wait()


def face_slab(ref, lead, layer):
    row = lax.broadcasted_iota(jnp.int32, (TW, TL), 0)
    slab = None
    for i in range(TW):
        line = jnp.broadcast_to(ref[lead + (i, slice(layer, layer + 1), slice(None))], (TW, TL))
        slab = line if slab is None else jnp.where(row == i, line, slab)
    return slab


def ghost_rows(low, high, c, h, x, scale):
    row = lax.broadcasted_iota(jnp.int32, (RING, TL), 0)
    tile = jnp.full((RING, TL), QUIET_STATE[c] if c < FIELDS else 1.0, jnp.float32)
    for d in range(DEPTH):
        line = high[c * DEPTH + d, h, pl.ds(x, 1), :] + CENTRE[c]
        tile = jnp.where(row == d, jnp.broadcast_to(line, (RING, TL)), tile)
        line = low[c * DEPTH + d, h, pl.ds(x, 1), :] + CENTRE[c]
        tile = jnp.where(row == RING - DEPTH + d, jnp.broadcast_to(line, (RING, TL)), tile)
    return tile * scale if c == FIELDS else tile


def slab_kernel(dims, refs):
    placed, from_low, from_high, _, x_low, x_high, layers, wide, edge, sems = refs
    nx, ny, nz = dims
    halves = nz // TL
    starts = (0, nx - DEPTH)
    loads = [
        pltpu.make_async_copy(placed.at[:, pl.ds(start, DEPTH)], edge.at[end], sems.at[end])
        for end, start in enumerate(starts)
    ]
    loads += [
        pltpu.make_async_copy(source, layers.at[k], sems.at[2 + k])
        for k, source in enumerate((from_low, from_high))
    ]
    for copy in loads:
        copy.start()
    for copy in loads:
        copy.wait()
    wide[...] = layers[...].astype(jnp.float32)
    low, high = wide.at[0], wide.at[1]
    size = halves * (ny + RING)
    for end, (out, start) in enumerate(((x_low, 0), (x_high, nx - DEPTH))):
        for c in range(FIELDS + 1):
            for d in range(DEPTH):
                parts = []
                for h in range(halves):
                    parts.append(edge[end, c, d, h])
                    parts.append(ghost_rows(low, high, c, h, start + d, TIME_STEP))
                block = jnp.concatenate(parts, axis=0) - CENTRE[c]
                number = c * DEPTH + d
                out[number * size : (number + 1) * size, :] = block.astype(jnp.bfloat16)


def primitives(u):
    density, m0, m1, m2, energy = u
    scaled = VISCOSITY / density
    f = [m0 * scaled, m1 * scaled, m2 * scaled]
    ratio = 0.5 / VISCOSITY
    n0, n1, n2 = ratio * m0, ratio * m1, ratio * m2
    d0, d1, d2 = n0 * f[0], n1 * f[1], n2 * f[2]
    c01, c02, c12 = n0 * f[1], n0 * f[2], n1 * f[2]
    kinetic = (d0 + d1) + d2
    hp = (0.5 * (HEAT_RATIO - 1.0)) * (energy - kinetic)
    f.append(scaled * (kinetic + (2.0 * CONDUCTION / VISCOSITY) * hp))
    enthalpy = ratio * energy + (1.0 / VISCOSITY) * hp
    flux = (
        (0.5 * m0, d0 + hp, c01, c02, enthalpy * f[0]),
        (0.5 * m1, c01, d1 + hp, c12, enthalpy * f[1]),
        (0.5 * m2, c02, c12, d2 + hp, enthalpy * f[2]),
    )
    return f, flux


def off_sections(dims, inputs, out_ref, scratch):
    placed, from_low, from_high, from_left, from_right = inputs
    out, layers, slabs, wide, begin, state_one, state_two, sems = scratch[:8]
    rings = scratch[8:]
    flux_x, flux_y, f_s = rings[:4], rings[4:8], rings[8:12]
    up_z, down_z = rings[12:16], rings[16:20]
    nx, ny, nz = dims
    halves = nz // TL
    rows = ny + RING
    main = FRONT + DEPTH
    load = pltpu.make_async_copy(
        placed, begin.at[:, pl.ds(main, nx), :, pl.ds(0, ny), :], sems.at[0]
    )
    low, high = wide.at[0], wide.at[1]
    received = [
        pltpu.make_async_copy(source, target, sems.at[1 + k])
        for k, (source, target) in enumerate(
            (
                (from_low, layers.at[0]),
                (from_high, layers.at[1]),
                (from_left, slabs.at[0]),
                (from_right, slabs.at[1]),
            )
        )
    ]
    lane = lax.broadcasted_iota(jnp.int32, (TW, TL), 1)
    first_lane, last_lane = lane == 0, lane == TL - 1

    def around_z(parts, distance, mask):
        rolled = [pltpu.roll(part, distance % TL, 1) for part in parts]
        return [jnp.where(mask, rolled[(h - distance) % halves], rolled[h]) for h in range(halves)]

    store = pltpu.make_async_copy(out, out_ref, sems.at[5])
    for copy in received + [load]:
        copy.start()
    yield
    for copy in received:
        copy.wait()
    wide[...] = layers[...].astype(jnp.float32)
    size = halves * rows
    for side, base in ((slabs.at[0], main - DEPTH), (slabs.at[1], main + nx)):
        for c in range(FIELDS + 1):
            for d in range(DEPTH):
                number = c * DEPTH + d
                block = side[number * size : (number + 1) * size, :].astype(jnp.float32)
                for h in range(halves):
                    begin[c, base + d, h] = block[h * rows : (h + 1) * rows] + CENTRE[c]

    def fill(x, _):
        for c in range(FIELDS + 1):
            for h in range(halves):
                begin[c, x + main, h, ny:rows, :] = ghost_rows(low, high, c, h, x, TIME_STEP)
        return 0

    lax.fori_loop(0, nx, fill, 0)
    load.wait()

    for section, (alpha, beta) in enumerate(SECTIONS):
        last = section == len(SECTIONS) - 1
        source, target = ((begin, state_one), (state_one, state_two), (state_two, out))[section]
        tiles = (ny if last else rows) // TW

        def step(i, turn):
            now, one, two, three = (turn % RINGS, *((turn - k) % RINGS for k in (1, 2, 3)))
            x = i - LAG
            for q in range(rows // TW):
                at = slice(q * TW, (q + 1) * TW)
                base = TW + q * TW
                here, after, before = (slice(base + k, base + k + TW) for k in (0, 1, -1))
                if q < tiles:
                    along_z = []
                    for b in range(FIELDS):
                        up = [up_z[two][b, h, at, :] for h in range(halves)]
                        down = [down_z[two][b, h, at, :] for h in range(halves)]
                        up = around_z(up, -1, last_lane)
                        down = around_z(down, 1, first_lane)
                        along_z.append([up[h] + down[h] for h in range(halves)])
                for h in range(halves):
                    for b in range(FIELDS):
                        if q >= tiles:
                            break
                        k = b - 1
                        rate = along_z[b][h] + (
                            (flux_x[three][b, h, at, :] - flux_x[one][b, h, at, :])
                            + (flux_y[two][b, h, before, :] - flux_y[two][b, h, after, :])
                        )
                        if b > 0:
                            sum_x = f_s[three][k, h, here, :] + f_s[one][k, h, here, :]
                            sum_y = f_s[two][k, h, before, :] + f_s[two][k, h, after, :]
                            rate = rate + ((sum_x + sum_y) - 6.0 * f_s[two][k, h, here, :])
                        moved = source[b, x, h, at, :] + begin[FIELDS, x, h, at, :] * rate
                        if section > 0:
                            moved = alpha * begin[b, x, h, at, :] + beta * moved
                        if last:
                            place = jnp.maximum(x - main, 0)
                            out[b, place, at, h * TL : (h + 1) * TL] = moved
                        else:
                            target[b, x, h, at, :] = moved
                    f, flux = primitives([source[c, i, h, at, :] for c in range(FIELDS)])
                    wrap = None
                    if q == 0:
                        wrap = slice(TW + rows, 2 * TW + rows)
                    if (q + 1) * TW == rows:
                        wrap = slice(0, TW)
                    for b in range(FIELDS):
                        if q < tiles:
                            flux_x[now][b, h, at, :] = flux[0][b]
                        flux_y[now][b, h, here, :] = flux[1][b]
                        if wrap is not None:
                            flux_y[now][b, h, wrap, :] = flux[1][b]
                        if b > 0:
                            f_s[now][b - 1, h, here, :] = f[b - 1]
                            if wrap is not None:
                                f_s[now][b - 1, h, wrap, :] = f[b - 1]
                    if q < tiles:
                        for b in range(FIELDS):
                            part = flux[2][b]
                            up_z[now][b, h, at, :] = f[b - 1] - part if b > 0 else -part
                            down_z[now][b, h, at, :] = f[b - 1] + part if b > 0 else part

        reach = DEPTH - 1 - section
        stop = main + nx + reach + LAG
        turns = -(-(nx + 2 * reach + LAG + 1) // RINGS)

        def body(j, _):
            for turn in range(RINGS):
                step(stop - turns * RINGS + j * RINGS + turn, turn)
            return 0

        lax.fori_loop(0, turns, body, 0)

    store.start()
    yield
    store.wait()
    yield


def find(table, count, slots, block):
    where_j, where_t = jnp.int32(0), jnp.int32(0)
    for j in range(count):
        for t in range(slots):
            hit = table[j * RING + 2 + t] == block
            where_j = jnp.where(hit, j, where_j)
            where_t = jnp.where(hit, t, where_t)
    return where_j, where_t


def pack_kernel(count, slots, refs):
    table, block_faces = refs[:2]
    held = refs[2 : 2 + count // 2]
    packed, sems = refs[4 + count // 2 :]
    for finish in (False, True):
        pack(count, slots, table, block_faces, held, packed, sems, finish)


def pack(count, slots, table, block_faces, held, packed, sems, finish):
    me = lax.axis_index("gy")
    offset = jnp.where(lax.rem(me, 2) == 1, 1, count - 1)
    for s in range(slots):
        block = table[offset * RING + 2 + s]

        @pl.when(block >= 0)
        def _():
            for side in range(2):
                j, t = find(table, count, slots, block_faces[side, block])
                number = s * 2 + side
                for m in range(count // 2):

                    @pl.when(j == 2 * m)
                    def _():
                        copy = pltpu.make_async_copy(
                            held[m].at[t * 2 + 1 - side], packed.at[number], sems.at[number]
                        )
                        if finish:
                            copy.wait()
                        else:
                            copy.start()


def near_sections(count, slots, dims, edges, inputs, out_ref, scratch):
    per_slot, around, normal = dims
    table, block_faces, slot_ref, near_ref, metric_ref = inputs[:5]
    parcels, rest = inputs[5 : 5 + count], inputs[5 + count :]
    if edges:
        held, packed, main_ref = rest[: count // 2], rest[count // 2], rest[count // 2 + 1]
    own = 2 * TW if edges else around
    rows = own + RING if edges else own
    begins, metrics, state_one, state_two, square, coeff, hold, out, along = scratch[:9]
    tile_buf, in_sems, out_sems, tile_sems = scratch[9:13]
    rings = scratch[13:37]
    flux_n, flux_a, f_s = rings[:4], rings[4:8], rings[8:12]
    up_s, down_s, own_s = rings[12:16], rings[16:20], rings[20:24]
    if edges:
        ghost, face_buf, main_buf, face_sems, main_sems = scratch[37:]
    lines = FIELDS * TW * TW
    wall = (-1.0, 1.0, 1.0, 1.0, -1.0)
    mirror = (-1.0, -1.0, -1.0, 1.0)
    pieces = ((0, 0), (around - TW, TW)) if edges else ((0, 0),)
    piece = TW if edges else around

    def loads(s):
        side = lax.rem(s, 2)
        return [
            pltpu.make_async_copy(
                ref.at[s, :, :, pl.ds(source, piece), :],
                buf.at[side, :, :, pl.ds(target, piece), :],
                in_sems.at[k, p, side],
            )
            for k, (ref, buf) in enumerate(((near_ref, begins), (metric_ref, metrics)))
            for p, (source, target) in enumerate(pieces)
        ]

    def main_loads(s):
        return [
            pltpu.make_async_copy(
                main_ref.at[s, :, :, pl.ds(source, TW), :],
                main_buf.at[s, :, :, pl.ds(target, TW), :],
                main_sems.at[s, p],
            )
            for p, (source, target) in enumerate(pieces)
        ]

    def stores(s):
        return [
            pltpu.make_async_copy(
                out.at[s, :, :, pl.ds(target, piece), :],
                out_ref.at[s, :, :, pl.ds(source, piece), :],
                out_sems.at[s, p],
            )
            for p, (source, target) in enumerate(pieces)
        ]

    def start_loads(s):
        @pl.when(slot_ref[s] >= 0)
        def _():
            for copy in loads(s):
                copy.start()

    start_loads(0)
    lane = lax.broadcasted_iota(jnp.int32, (rows, TL), 1)
    tile_loads = [
        pltpu.make_async_copy(
            parcels[j].at[pl.ds(lines, lines), :], tile_buf.at[j], tile_sems.at[j]
        )
        for j in range(count)
    ]
    for copy in tile_loads:
        copy.start()

    def face_loads(s):
        for side in range(2):
            j, t = find(table, count, slots, block_faces[side, slot_ref[s]])
            target, sem = face_buf.at[s, side], face_sems.at[s, side]
            for m in range(count // 2):

                @pl.when(j == 2 * m)
                def _():
                    pltpu.make_async_copy(held[m].at[t * 2 + 1 - side], target, sem).start()

            @pl.when(lax.rem(j, 2) == 1)
            def _():
                pltpu.make_async_copy(packed.at[s * 2 + side], target, sem).start()

    if edges:
        for s in range(slots):

            @pl.when(slot_ref[s] >= 0)
            def _():
                face_loads(s)
                for copy in main_loads(s):
                    copy.start()

    yield
    row = lax.broadcasted_iota(jnp.int32, (RING, TL), 0)

    def take_ghosts(s, begin, metric):
        for side in range(2):
            pltpu.make_async_copy(
                packed.at[0], face_buf.at[s, side], face_sems.at[s, side]
            ).wait()
            ghost[side] = face_buf[s, side].astype(jnp.float32)

        def ghost_tile(number, layers, i, fill, centre):
            tile = jnp.full((RING, TL), fill, jnp.float32)
            for d in range(layers):
                at = (number + d) * TW + i
                line = jnp.broadcast_to(ghost[1, at : at + 1, :] + centre, (RING, TL))
                tile = jnp.where(row == d, line, tile)
                line = jnp.broadcast_to(ghost[0, at : at + 1, :] + centre, (RING, TL))
                tile = jnp.where(row == RING - layers + d, line, tile)
            return tile

        step = DEPTH - 1
        for i in range(normal):
            for c in range(FIELDS):
                begin[c, i, own:rows, :] = ghost_tile(
                    c * DEPTH, DEPTH, i, QUIET_STATE[c], CENTRE[c]
                )
            for a in range(3):
                metric[a, i, own:rows, :] = ghost_tile(
                    FIELDS * DEPTH + a * step, step, i, 1.0, 0.0
                )
        last_layer = (FACE_LAYERS - 1) * TW
        hold[own:rows, :] = TIME_STEP * jnp.where(
            row < RING // 2,
            ghost[1, last_layer : last_layer + TW, :],
            ghost[0, last_layer : last_layer + TW, :],
        )

    def slot_work(s, _):
        begin, metric = begins.at[lax.rem(s, 2)], metrics.at[lax.rem(s, 2)]

        @pl.when(s + 1 < slots)
        def _():
            start_loads(jnp.minimum(s + 1, slots - 1))

        if not edges:

            @pl.when(slot_ref[s] < 0)
            def _():
                out[s] = jnp.zeros(out.shape[1:], jnp.float32)

        @pl.when(slot_ref[s] >= 0)
        def _():
            if edges:
                take_ghosts(s, begin, metric)
            hold[0:own, :] = jnp.full((own, TL), TIME_STEP, jnp.float32)
            for copy in loads(s):
                copy.wait()
            if edges:
                for copy in main_loads(s):
                    copy.wait()

            for j in range(count):
                tile = table[j * RING + 1]
                number = tile % per_slot
                mine = (tile >= 0) & (tile // per_slot == s)
                if edges:
                    mine = mine & ((number == 0) | (number == per_slot - 1))
                    number = jnp.where(number == 0, 0, 1)

                @pl.when(mine)
                def _():
                    q = aligned(number, TW)
                    for c in range(FIELDS):
                        for i in range(0, TW, 2):
                            start = (c * TW + i) * TW
                            pair = tile_buf[j, start : start + 2 * TW, :].astype(jnp.float32)
                            begin[c, i, pl.ds(q, TW), :] = pair[:TW]
                            begin[c, i + 1, pl.ds(q, TW), :] = pair[TW:]
                    hold[pl.ds(q, TW), :] = jnp.zeros((TW, TL), jnp.float32)

            def prepare(i, _):
                squares = [metric[a, i] * metric[a, i] for a in range(3)]
                for a in range(2):
                    square[a, i] = squares[a]
                total = -2.0 * ((squares[0] + squares[1]) + squares[2])
                at_end = (lane == 0) | (lane == TL - 1)
                coeff[i] = jnp.where(at_end, total + squares[2], total)
                g = metric[2, i]
                along[0, i] = jnp.where(lane == 0, 0.0, pltpu.roll(g, 1, 1))
                along[1, i] = jnp.where(lane == TL - 1, 0.0, pltpu.roll(g, TL - 1, 1))
                along[2, i] = jnp.where(lane == 0, g, jnp.where(lane == TL - 1, -g, 0.0))
                return 0

            lax.fori_loop(0, normal, prepare, 0)

            for section, (alpha, beta) in enumerate(SECTIONS):
                last = section == len(SECTIONS) - 1
                source = (begin, state_one, state_two)[section]
                target = (state_one, state_two, out)[section]
                tiles = (own if last else rows) // TW

                def advance(x, q):
                    at = slice(q * TW, (q + 1) * TW)
                    base = TW + q * TW
                    here, after, before = (slice(base + k, base + k + TW) for k in (0, 1, -1))
                    mid, low = x % RINGS, (x - 1) % RINGS
                    high = (x + 1) % RINGS
                    g = [metric[a, x, at, :] for a in range(2)]
                    g2 = [square[a, x, at, :] for a in range(2)]
                    center = coeff[x, at, :]
                    for b in range(FIELDS):
                        k = b - 1
                        rate = pltpu.roll(up_s[mid][b, at, :], TL - 1, 1)
                        rate = rate + pltpu.roll(down_s[mid][b, at, :], 1, 1)
                        rate = rate + own_s[mid][b, at, :]
                        rate = rate + g[0] * (flux_n[low][b, at, :] - flux_n[high][b, at, :])
                        rate = rate + g[1] * (
                            flux_a[mid][b, before, :] - flux_a[mid][b, after, :]
                        )
                        if b > 0:
                            rate = rate + g2[0] * (f_s[low][k, here, :] + f_s[high][k, here, :])
                            rate = rate + g2[1] * (
                                f_s[mid][k, before, :] + f_s[mid][k, after, :]
                            )
                            rate = rate + center * f_s[mid][k, here, :]
                        moved = source[b, x, at, :] + hold[at, :] * rate
                        if section > 0:
                            moved = alpha * begin[b, x, at, :] + beta * moved
                        if last and edges:
                            right = row < DEPTH if q == 0 else row >= TW - DEPTH
                            moved = jnp.where(right, moved, main_buf[s, b, x, at, :])
                        if last:
                            out[s, b, x, at, :] = moved
                        else:
                            target[b, x, at, :] = moved

                def work(i, q):
                    at = slice(q * TW, (q + 1) * TW)
                    base = TW + q * TW
                    here = slice(base, base + TW)
                    now = i % RINGS
                    f, flux = primitives([source[c, i, at, :] for c in range(FIELDS)])
                    wrap = None
                    if q == 0:
                        wrap = slice(TW + rows, 2 * TW + rows)
                    if base == rows:
                        wrap = slice(0, TW)
                    for b in range(FIELDS):
                        if q < tiles:
                            flux_n[now][b, at, :] = flux[0][b]
                            if i == 0:
                                flux_n[now - 1][b, at, :] = wall[b] * flux[0][b]
                            if i == normal - 1:
                                flux_n[(now + 1) % RINGS][b, at, :] = flux[0][b]
                        flux_a[now][b, here, :] = flux[1][b]
                        if wrap is not None:
                            flux_a[now][b, wrap, :] = flux[1][b]
                        if b > 0:
                            f_s[now][b - 1, here, :] = f[b - 1]
                            if wrap is not None:
                                f_s[now][b - 1, wrap, :] = f[b - 1]
                            if i == 0:
                                f_s[now - 1][b - 1, here, :] = mirror[b - 1] * f[b - 1]
                            if i == normal - 1:
                                f_s[(now + 1) % RINGS][b - 1, here, :] = f[b - 1]
                    if q < tiles:
                        g_up, g_down = along[0, i, at, :], along[1, i, at, :]
                        g_own = along[2, i, at, :]
                        for b in range(FIELDS):
                            part = flux[2][b]
                            if b > 0:
                                up_s[now][b, at, :] = g_up * (g_up * f[b - 1] - part)
                                down_s[now][b, at, :] = g_down * (g_down * f[b - 1] + part)
                            else:
                                up_s[now][b, at, :] = -(g_up * part)
                                down_s[now][b, at, :] = g_down * part
                            own_s[now][b, at, :] = g_own * part

                for i in range(normal + LAG):
                    for q in range(rows // TW):
                        if i >= LAG and q < tiles:
                            advance(i - LAG, q)
                        if i < normal:
                            work(i, q)

        def send_out():
            for copy in stores(s):
                copy.start()

        if edges:
            pl.when(slot_ref[s] >= 0)(send_out)
        else:
            send_out()
        return 0

    for copy in tile_loads:
        copy.wait()
    lax.fori_loop(0, slots, slot_work, 0)
    yield
    for s in range(slots):

        def end_out():
            for copy in stores(s):
                copy.wait()

        if edges:
            pl.when(slot_ref[s] >= 0)(end_out)
        else:
            end_out()
    yield


def near_kernel(count, slots, dims, refs):
    inputs, (out_ref, token) = refs[: 5 + count], refs[6 + count : 8 + count]
    token[...] = jnp.zeros(token.shape, jnp.float32)
    for _ in near_sections(count, slots, dims, False, inputs, out_ref, refs[8 + count :]):
        pass


def edge_kernel(count, slots, dims, refs):
    size = 5 + count + count // 2 + 2
    out_ref, scratch = refs[size + 1], refs[size + 2 :]
    for _ in near_sections(count, slots, dims, True, refs[:size], out_ref, scratch):
        pass


def off_kernel(dims, refs):
    out_ref, token = refs[6:8]
    token[...] = jnp.zeros(token.shape, jnp.float32)
    for _ in off_sections(dims, refs[:5], out_ref, refs[8:]):
        pass


def packed_refs(kernel, *first):
    def body(*refs):
        kernel(*first, refs)

    return body


def off_buffers(dims, layer_shape, slab_shape):
    nx, ny, nz = dims
    halves, rows = nz // TL, ny + RING
    f32, half = jnp.float32, jnp.bfloat16
    slices = FRONT + nx + 2 * DEPTH + 2
    return (
        [
            VMEM((FIELDS, nx, ny, nz), f32),
            VMEM((2,) + layer_shape, half),
            VMEM((2,) + slab_shape, half),
            VMEM((2,) + layer_shape, f32),
            VMEM((FIELDS + 1, slices, halves, rows, TL), f32),
            VMEM((FIELDS, slices, halves, rows, TL), f32),
            VMEM((FIELDS, slices, halves, rows, TL), f32),
            pltpu.SemaphoreType.DMA((6,)),
        ]
        + [VMEM((FIELDS, halves, rows, TL), f32)] * RINGS
        + [VMEM((FIELDS, halves, rows + 2 * TW, TL), f32)] * RINGS
        + [VMEM((FIELDS - 1, halves, rows + 2 * TW, TL), f32)] * RINGS
        + [VMEM((FIELDS, halves, rows, TL), f32)] * RINGS * 2
    )


def near_buffers(count, slots, dims, edges):
    _, around, normal = dims
    f32, dma = jnp.float32, pltpu.SemaphoreType.DMA
    own = 2 * TW if edges else around
    rows = own + RING if edges else own
    pieces = 2 if edges else 1
    extra = []
    if edges:
        extra = [
            VMEM((2, FACE_ROWS, TL), f32),
            VMEM((slots, 2, FACE_ROWS, TL), jnp.bfloat16),
            VMEM((slots, FIELDS, normal, own, TL), f32),
            dma((slots, 2)),
            dma((slots, 2)),
        ]
    return (
        [
            VMEM((2, FIELDS, normal, rows, TL), f32),
            VMEM((2, 3, normal, rows, TL), f32),
            VMEM((FIELDS, normal, rows, TL), f32),
            VMEM((FIELDS, normal, rows, TL), f32),
            VMEM((2, normal, rows, TL), f32),
            VMEM((normal, rows, TL), f32),
            VMEM((rows, TL), f32),
            VMEM((slots, FIELDS, normal, own, TL), f32),
            VMEM((3, normal, rows, TL), f32),
            VMEM((count, FIELDS * TW * TW, TL), jnp.bfloat16),
            dma((2, pieces, 2)),
            dma((slots, pieces)),
            dma((count,)),
        ]
        + [VMEM((FIELDS, rows, TL), f32)] * RINGS
        + [VMEM((FIELDS, rows + 2 * TW, TL), f32)] * RINGS
        + [VMEM((FIELDS - 1, rows + 2 * TW, TL), f32)] * RINGS
        + [VMEM((FIELDS, rows, TL), f32)] * RINGS * 3
        + extra
    )


def ring(axis, distance):
    count = lax.axis_size(axis)
    return [(i, (i + distance) % count) for i in range(count)]


def send(value, axis, distance):
    return lax.ppermute(value, axis, ring(axis, distance))


def local(
    off_state,
    near_state,
    near_metric,
    slot_block,
    block_faces,
    fringe_in,
    fringe_in_maps,
    fringe_out,
    fringe_out_maps,
):
    count = lax.axis_size("gy")
    slots, _, normal, around, span = near_state.shape
    _, nx, ny, nz = off_state.shape
    rows_here = fringe_in.shape[1]
    per_slot = around // TW
    lines = FIELDS * TW * TW
    half, f32 = jnp.bfloat16, jnp.float32
    shape = jax.ShapeDtypeStruct
    block_faces = block_faces.T
    tile_buf = VMEM((count, FIELDS, TW, TW, TL), f32)
    map_buf = VMEM((count, TL, TL), half)

    parcels = pl.pallas_call(
        packed_refs(
            interp_kernel, count, slots, (rows_here, per_slot, ny // TW, nz // TL)
        ),
        out_shape=[shape((2 * lines + META, TL), half)] * count,
        in_specs=[smem_spec()] * 3 + [any_spec()] * 4,
        out_specs=[vmem_spec()] * count,
        scratch_shapes=[
            tile_buf,
            tile_buf,
            map_buf,
            map_buf,
            pltpu.SemaphoreType.DMA((4, count)),
        ],
        compiler_params=params(VMEM_MIB),
        cost_estimate=cost(2e8, 6e6),
        name="interp",
    )(fringe_in, fringe_out, slot_block, off_state, near_state, fringe_in_maps, fringe_out_maps)
    dma = pltpu.SemaphoreType.DMA
    planes = (FIELDS + 1) * DEPTH
    halves = nz // TL
    layer_shape = (planes, halves, nx, TL)
    base_layers, base_faces, base_placed = pl.pallas_call(
        packed_refs(base_kernel, slots, (around, nx, ny, nz)),
        out_shape=[
            shape((2,) + layer_shape, f32),
            shape((2 * slots, FACE_ROWS, TL), f32),
            shape((FIELDS + 1, nx, halves, ny, TL), f32),
        ],
        in_specs=[vmem_spec()] + [any_spec()] * 2,
        out_specs=[vmem_spec()] * 3,
        scratch_shapes=[
            VMEM((2, slots, FIELDS, normal, TW, TL), f32),
            VMEM((2, slots, 3, normal, TW, TL), f32),
            dma((2, 2)),
        ],
        compiler_params=params(VMEM_MIB),
        cost_estimate=cost(1e7, 2e7),
        name="base",
    )(off_state, near_state, near_metric)

    parcels = [parcels[0]] + [send(parcels[j], "gy", j) for j in range(1, count)]

    y_low, y_high, faces, table, placed = pl.pallas_call(
        packed_refs(patch_kernel, count, per_slot, (nx, ny, nz)),
        out_shape=[
            shape(layer_shape, half),
            shape(layer_shape, half),
            shape((2 * slots, FACE_ROWS, TL), half),
            shape((count * RING,), jnp.int32),
            shape(base_placed.shape, f32),
        ],
        in_specs=[any_spec()] * (count + 3),
        out_specs=[vmem_spec()] * 3 + [smem_spec(), any_spec()],
        input_output_aliases={count + 2: 4},
        scratch_shapes=[
            VMEM((2,) + layer_shape, f32),
            VMEM((2 * slots, FACE_ROWS, TL), f32),
            VMEM((count, 2 * lines + META, TL), half),
            VMEM((count, lines, TL), f32),
            VMEM((lines, TL), f32),
            VMEM((TW, TW, TL), f32),
            VMEM((count * META, TL), jnp.int32),
            SMEM((count * META, TL), jnp.int32),
            dma((2 * count + 3,)),
            dma((2, count)),
        ],
        compiler_params=params(VMEM_MIB),
        cost_estimate=cost(1e7, 8e6),
        name="patch",
    )(*parcels, base_layers, base_faces, base_placed)

    held = [faces] + [send(faces, "gy", 2 * m) for m in range(1, count // 2)]
    from_low = send(y_high, "gy", 1)
    from_high = send(y_low, "gy", count - 1)

    near_dims, off_dims = (per_slot, around, normal), (nx, ny, nz)
    near_inputs = (table, block_faces, slot_block, near_state, near_metric, *parcels)
    token_shape = shape((RING, TL), f32)

    near_main, token = pl.pallas_call(
        packed_refs(near_kernel, count, slots, near_dims),
        out_shape=[shape(near_state.shape, f32), token_shape],
        in_specs=[smem_spec()] * 3 + [any_spec()] * (2 + count + 1),
        out_specs=[any_spec(), vmem_spec()],
        scratch_shapes=near_buffers(count, slots, near_dims, False),
        compiler_params=params(VMEM_MIB),
        cost_estimate=cost(1e8, 5e7),
        name="near_sections",
    )(*near_inputs, faces)

    x_low, x_high = pl.pallas_call(
        packed_refs(slab_kernel, off_dims),
        out_shape=[shape((planes * halves * (ny + RING), TL), half)] * 2,
        in_specs=[any_spec()] * 4,
        out_specs=[vmem_spec()] * 2,
        scratch_shapes=[
            VMEM((2,) + layer_shape, half),
            VMEM((2,) + layer_shape, f32),
            VMEM((2, FIELDS + 1, DEPTH, halves, ny, TL), f32),
            dma((4,)),
        ],
        compiler_params=params(VMEM_MIB),
        cost_estimate=cost(1e6, 4e6),
        name="slabs",
    )(placed, from_low, from_high, token)
    from_left = send(x_high, "gx", 1)
    from_right = send(x_low, "gx", lax.axis_size("gx") - 1)

    packed_here = pl.pallas_call(
        packed_refs(pack_kernel, count, slots),
        out_shape=shape((2 * slots, FACE_ROWS, TL), half),
        in_specs=[smem_spec()] * 2 + [any_spec()] * (count // 2 + 2),
        out_specs=vmem_spec(),
        scratch_shapes=[dma((2 * slots,))],
        compiler_params=params(VMEM_MIB),
        cost_estimate=cost(1e5, 2e6),
        name="pack",
    )(table, block_faces, *held, from_left, from_right)
    packed = lax.ppermute(packed_here, "gy", [(i, i ^ 1) for i in range(count)])

    off_next, token = pl.pallas_call(
        packed_refs(off_kernel, off_dims),
        out_shape=[shape(off_state.shape, f32), token_shape],
        in_specs=[any_spec()] * 6,
        out_specs=[any_spec(), vmem_spec()],
        scratch_shapes=off_buffers(off_dims, layer_shape, x_low.shape),
        compiler_params=params(VMEM_MIB),
        cost_estimate=cost(1e8, 5e7),
        name="off_sections",
    )(placed, from_low, from_high, from_left, from_right, packed_here)

    number = len(near_inputs) + count // 2 + 1
    near_next = pl.pallas_call(
        packed_refs(edge_kernel, count, slots, near_dims),
        out_shape=shape(near_state.shape, f32),
        in_specs=[smem_spec()] * 3 + [any_spec()] * (number - 2 + 1),
        out_specs=any_spec(),
        input_output_aliases={number: 0},
        scratch_shapes=near_buffers(count, slots, near_dims, True),
        compiler_params=params(VMEM_MIB),
        cost_estimate=cost(1e8, 5e7),
        name="near_edges",
    )(*near_inputs, *held, packed, near_main, token)
    return off_next, near_next


def solution(mesh):
    in_specs = (
        P(None, "gx", "gy", None),
        P(("gx", "gy"), None, None, None, None),
        P(("gx", "gy"), None, None, None, None),
        P(("gx", "gy")),
        P(),
        P(None, ("gx", "gy")),
        P(("gx", "gy"), None, None),
        P(None, ("gx", "gy")),
        P(("gx", "gy"), None, None),
    )
    out_specs = (P(None, "gx", "gy", None), P(("gx", "gy"), None, None, None, None))
    return jax.shard_map(local, mesh=mesh, in_specs=in_specs, out_specs=out_specs, check_vma=False)
```

```python
import functools

import jax
import jax.numpy as jnp
from jax import lax
from jax.experimental import pallas as pl
from jax.experimental.pallas import tpu as pltpu
from jax.sharding import PartitionSpec as P

TW = 8
TL = 128
DEPTH = 3
RING = 8
META = 16
FIELDS = 5
HEAT_RATIO = 1.4
VISCOSITY = 0.8
CONDUCTION = 1.12
TIME_STEP = 0.1
QUIET_STATE = (1.0, 0.0, 0.0, 0.0, 2.5)
CENTRE = (1.0, 0.0, 0.0, 0.0, 2.5, 0.0)
SECTIONS = ((0.0, 1.0), (0.75, 0.25), (1.0 / 3.0, 2.0 / 3.0))
FACE_LAYERS = FIELDS * DEPTH + 3 * (DEPTH - 1) + 1
FACE_ROWS = FACE_LAYERS * TW
LAG = 2
RINGS = 4
VMEM_MIB = 61
FRONT = 6

VMEM = pltpu.VMEM
SMEM = pltpu.SMEM


def vmem_spec():
    return pl.BlockSpec(memory_space=VMEM)


def smem_spec():
    return pl.BlockSpec(memory_space=SMEM)


def any_spec():
    return pl.BlockSpec(memory_space=pl.ANY)


def params(mebibytes):
    return pltpu.CompilerParams(vmem_limit_bytes=mebibytes * 1024 * 1024)


def cost(flops, moved):
    return pl.CostEstimate(flops=int(flops), bytes_accessed=int(moved), transcendentals=0)


def aligned(value, unit):
    return pl.multiple_of(value * unit, unit)


def off_place(tile, y_tiles, z_tiles):
    a = tile // (y_tiles * z_tiles)
    b = (tile // z_tiles) % y_tiles
    c = tile % z_tiles
    return aligned(a, TW), aligned(b, TW), aligned(c, TL)


def interp_kernel(count, slots, dims, refs):
    (fin, fout, slot_ref, off_ref, near_ref, maps_in, maps_out) = refs[:7]
    outs = refs[7 : 7 + count]
    near_buf, off_buf, in_buf, out_buf, sems = refs[7 + count :]
    rows_here, per_slot, y_tiles, z_tiles = dims
    me = lax.axis_index("gy")
    copies, heads = [], []
    for j in range(count):
        dest = lax.rem(me + j, count)
        k_in, k_out = jnp.int32(0), jnp.int32(0)
        t_in, t_out = jnp.int32(-1), jnp.int32(-1)
        for k in range(rows_here):
            hit = fin[1, k] == dest
            k_in = jnp.where(hit, k, k_in)
            t_in = jnp.where(hit, fin[2, k], t_in)
            hit = fout[1, k] == dest
            k_out = jnp.where(hit, k, k_out)
            t_out = jnp.where(hit, fout[2, k], t_out)
        heads.append((t_in, t_out))
        donor = fin[0, k_in]
        slot, q = donor // per_slot, aligned(donor % per_slot, TW)
        x0, y0, z0 = off_place(fout[0, k_out], y_tiles, z_tiles)
        group = [
            pltpu.make_async_copy(
                near_ref.at[slot, :, :, pl.ds(q, TW), :], near_buf.at[j], sems.at[0, j]
            ),
            pltpu.make_async_copy(maps_in.at[k_in], in_buf.at[j], sems.at[1, j]),
            pltpu.make_async_copy(
                off_ref.at[:, pl.ds(x0, TW), pl.ds(y0, TW), pl.ds(z0, TL)],
                off_buf.at[j],
                sems.at[2, j],
            ),
            pltpu.make_async_copy(maps_out.at[k_out], out_buf.at[j], sems.at[3, j]),
        ]
        for copy in group:
            copy.start()
        copies.append(group)
    lines = FIELDS * TW * TW
    row = lax.broadcasted_iota(jnp.int32, (META, TL), 0)
    for j in range(count):
        for copy in copies[j]:
            copy.wait()
        for side, (tiles, maps) in enumerate(((near_buf, in_buf), (off_buf, out_buf))):
            donors = tiles[j].reshape(lines, TL).astype(jnp.bfloat16)
            mixed = jnp.dot(donors, maps[j], preferred_element_type=jnp.float32)
            outs[j][side * lines : (side + 1) * lines, :] = mixed.astype(jnp.bfloat16)
        head = jnp.where(row == 0, heads[j][0], jnp.where(row == 1, heads[j][1], 0))
        for s in range(slots):
            head = jnp.where(row == 2 + s, slot_ref[s], head)
        outs[j][2 * lines :, :] = head.astype(jnp.float32).astype(jnp.bfloat16)


def base_kernel(slots, dims, refs):
    off_ref, near_ref, metric_ref, layers, faces, placed, edge, medge, sems = refs
    around, nx, ny, nz = dims
    loads = []
    for end, start in enumerate((0, around - TW)):
        for k, (source, target) in enumerate(((near_ref, edge), (metric_ref, medge))):
            loads.append(
                pltpu.make_async_copy(
                    source.at[:, :, :, pl.ds(start, TW), :], target.at[end], sems.at[k, end]
                )
            )
    for copy in loads:
        copy.start()

    for h in range(nz // TL):
        placed[0:FIELDS, :, h] = off_ref[:, :, :, h * TL : (h + 1) * TL]
    placed[FIELDS] = jnp.full(placed.shape[1:], TIME_STEP, jnp.float32)

    def turn(x, _):
        for end, start in enumerate((0, ny - DEPTH)):
            for c in range(FIELDS):
                for d in range(DEPTH):
                    for h in range(nz // TL):
                        layers[end, c * DEPTH + d, h, pl.ds(x, 1), :] = (
                            off_ref[c, x, start + d : start + d + 1, h * TL : (h + 1) * TL]
                            - CENTRE[c]
                        )
        return 0

    lax.fori_loop(0, nx, turn, 0)
    layers[:, FIELDS * DEPTH :] = jnp.ones((2, DEPTH) + layers.shape[2:], jnp.float32)
    for copy in loads:
        copy.wait()
    for s in range(slots):
        for end in range(2):
            number = 0
            for c in range(FIELDS):
                for d in range(DEPTH):
                    layer = d + (0 if end == 0 else TW - DEPTH)
                    slab = face_slab(edge, (end, s, c), layer) - CENTRE[c]
                    faces[s * 2 + end, number * TW : (number + 1) * TW, :] = slab
                    number += 1
            for a in range(3):
                for d in range(DEPTH - 1):
                    layer = d + (0 if end == 0 else TW - DEPTH + 1)
                    slab = face_slab(medge, (end, s, a), layer)
                    faces[s * 2 + end, number * TW : (number + 1) * TW, :] = slab
                    number += 1
            faces[s * 2 + end, number * TW : (number + 1) * TW, :] = jnp.ones(
                (TW, TL), jnp.float32
            )


def patch_kernel(count, per_slot, dims, refs):
    parcels = refs[:count]
    base_layers, base_faces, _, y_low, y_high, faces, table, placed = refs[count : count + 8]
    layers, front, tiles, wide, near_wide, nothing, head_v, head_s, sems, out_sems = refs[count + 8 :]
    nx, ny, nz = dims
    y_tiles, z_tiles = ny // TW, nz // TL
    lines = FIELDS * TW * TW
    heads = [
        pltpu.make_async_copy(
            parcels[j].at[pl.ds(2 * lines, META), :],
            tiles.at[j, pl.ds(2 * lines, META), :],
            sems.at[j],
        )
        for j in range(count)
    ]
    bodies = [
        pltpu.make_async_copy(
            parcels[j].at[pl.ds(0, 2 * lines), :],
            tiles.at[j, pl.ds(0, 2 * lines), :],
            sems.at[count + j],
        )
        for j in range(count)
    ]
    rest = [
        pltpu.make_async_copy(base_layers, layers, sems.at[2 * count]),
        pltpu.make_async_copy(base_faces, front, sems.at[2 * count + 1]),
    ]
    for copy in heads + bodies + rest:
        copy.start()
    nothing[...] = jnp.zeros(nothing.shape, jnp.float32)
    for j in range(count):
        heads[j].wait()
        head = tiles[j, 2 * lines :, :].astype(jnp.float32)
        head_v[j * META : (j + 1) * META, :] = head.astype(jnp.int32)
    head_copy = pltpu.make_async_copy(head_v, head_s, sems.at[2 * count + 2])
    head_copy.start()
    for j in range(count):
        bodies[j].wait()
        wide[j] = tiles[j, :lines, :].astype(jnp.float32)
    for copy in rest:
        copy.wait()
    head_copy.wait()
    for j in range(count):
        for r in range(RING):
            table[j * RING + r] = head_s[j * META + r, 0]

    def tile_place(j):
        tile = head_s[j * META, 0]
        a = tile // (y_tiles * z_tiles)
        b = (tile // z_tiles) % y_tiles
        return tile, aligned(a, TW), b, tile % z_tiles

    def tile_copies(j):
        tile, x0, b, h = tile_place(j)
        at = (pl.ds(x0, TW), h, pl.ds(aligned(b, TW), TW), slice(None))
        return [
            pltpu.make_async_copy(
                wide.at[j].reshape(FIELDS, TW, TW, TL),
                placed.at[(pl.ds(0, FIELDS),) + at],
                out_sems.at[0, j],
            ),
            pltpu.make_async_copy(nothing, placed.at[(FIELDS,) + at], out_sems.at[1, j]),
        ]

    for j in range(count):
        tile, x0, b, h = tile_place(j)

        @pl.when(tile >= 0)
        def _():
            for copy in tile_copies(j):
                copy.start()

        for end, edge_tile in enumerate((0, y_tiles - 1)):

            @pl.when((tile >= 0) & (b == edge_tile))
            def _():
                first = 0 if end == 0 else TW - DEPTH
                for c in range(FIELDS):
                    for d in range(DEPTH):
                        slab = wide[j, pl.ds(c * TW * TW + first + d, TW, stride=TW), :]
                        layers[end, c * DEPTH + d, h, pl.ds(x0, TW), :] = slab - CENTRE[c]
                for d in range(DEPTH):
                    layers[end, FIELDS * DEPTH + d, h, pl.ds(x0, TW), :] = jnp.zeros(
                        (TW, TL), jnp.float32
                    )

        tile = head_s[j * META + 1, 0]
        s = tile // per_slot
        for end, edge_tile in enumerate((0, per_slot - 1)):

            @pl.when((tile >= 0) & (tile % per_slot == edge_tile))
            def _():
                near_wide[...] = tiles[j, lines : 2 * lines, :].astype(jnp.float32)
                first = 0 if end == 0 else TW - DEPTH
                for c in range(FIELDS):
                    for d in range(DEPTH):
                        slab = near_wide[pl.ds(c * TW * TW + first + d, TW, stride=TW), :]
                        number = c * DEPTH + d
                        front[s * 2 + end, number * TW : (number + 1) * TW, :] = slab - CENTRE[c]
                front[s * 2 + end, FACE_ROWS - TW :, :] = jnp.zeros((TW, TL), jnp.float32)

    for end, out in enumerate((y_low, y_high)):
        out[...] = layers[end].astype(jnp.bfloat16)
    faces[...] = front[...].astype(jnp.bfloat16)
    for j in range(count):

        @pl.when(head_s[j * META, 0] >= 0)
        def _():
            for copy in tile_copies(j):
                copy.wait()


def face_slab(ref, lead, layer):
    row = lax.broadcasted_iota(jnp.int32, (TW, TL), 0)
    slab = None
    for i in range(TW):
        line = jnp.broadcast_to(ref[lead + (i, slice(layer, layer + 1), slice(None))], (TW, TL))
        slab = line if slab is None else jnp.where(row == i, line, slab)
    return slab


def ghost_rows(low, high, c, h, x, scale):
    row = lax.broadcasted_iota(jnp.int32, (RING, TL), 0)
    tile = jnp.full((RING, TL), QUIET_STATE[c] if c < FIELDS else 1.0, jnp.float32)
    for d in range(DEPTH):
        line = high[c * DEPTH + d, h, pl.ds(x, 1), :] + CENTRE[c]
        tile = jnp.where(row == d, jnp.broadcast_to(line, (RING, TL)), tile)
        line = low[c * DEPTH + d, h, pl.ds(x, 1), :] + CENTRE[c]
        tile = jnp.where(row == RING - DEPTH + d, jnp.broadcast_to(line, (RING, TL)), tile)
    return tile * scale if c == FIELDS else tile


def slab_kernel(dims, refs):
    placed, from_low, from_high, _, x_low, x_high, layers, wide, edge, sems = refs
    nx, ny, nz = dims
    halves = nz // TL
    starts = (0, nx - DEPTH)
    loads = [
        pltpu.make_async_copy(placed.at[:, pl.ds(start, DEPTH)], edge.at[end], sems.at[end])
        for end, start in enumerate(starts)
    ]
    loads += [
        pltpu.make_async_copy(source, layers.at[k], sems.at[2 + k])
        for k, source in enumerate((from_low, from_high))
    ]
    for copy in loads:
        copy.start()
    for copy in loads:
        copy.wait()
    wide[...] = layers[...].astype(jnp.float32)
    low, high = wide.at[0], wide.at[1]
    size = halves * (ny + RING)
    for end, (out, start) in enumerate(((x_low, 0), (x_high, nx - DEPTH))):
        for c in range(FIELDS + 1):
            for d in range(DEPTH):
                parts = []
                for h in range(halves):
                    parts.append(edge[end, c, d, h])
                    parts.append(ghost_rows(low, high, c, h, start + d, TIME_STEP))
                block = jnp.concatenate(parts, axis=0) - CENTRE[c]
                number = c * DEPTH + d
                out[number * size : (number + 1) * size, :] = block.astype(jnp.bfloat16)


def primitives(u):
    density, m0, m1, m2, energy = u
    scaled = VISCOSITY / density
    f = [m0 * scaled, m1 * scaled, m2 * scaled]
    ratio = 0.5 / VISCOSITY
    n0, n1, n2 = ratio * m0, ratio * m1, ratio * m2
    d0, d1, d2 = n0 * f[0], n1 * f[1], n2 * f[2]
    c01, c02, c12 = n0 * f[1], n0 * f[2], n1 * f[2]
    kinetic = (d0 + d1) + d2
    hp = (0.5 * (HEAT_RATIO - 1.0)) * (energy - kinetic)
    f.append(scaled * (kinetic + (2.0 * CONDUCTION / VISCOSITY) * hp))
    enthalpy = ratio * energy + (1.0 / VISCOSITY) * hp
    flux = (
        (0.5 * m0, d0 + hp, c01, c02, enthalpy * f[0]),
        (0.5 * m1, c01, d1 + hp, c12, enthalpy * f[1]),
        (0.5 * m2, c02, c12, d2 + hp, enthalpy * f[2]),
    )
    return f, flux


def off_sections(dims, inputs, out_ref, scratch):
    placed, from_low, from_high, from_left, from_right = inputs
    out, layers, slabs, wide, begin, state_one, state_two, sems = scratch[:8]
    rings = scratch[8:]
    flux_x, flux_y, f_s = rings[:4], rings[4:8], rings[8:12]
    up_z, down_z = rings[12:16], rings[16:20]
    nx, ny, nz = dims
    halves = nz // TL
    rows = ny + RING
    main = FRONT + DEPTH
    load = pltpu.make_async_copy(
        placed, begin.at[:, pl.ds(main, nx), :, pl.ds(0, ny), :], sems.at[0]
    )
    low, high = wide.at[0], wide.at[1]
    received = [
        pltpu.make_async_copy(source, target, sems.at[1 + k])
        for k, (source, target) in enumerate(
            (
                (from_low, layers.at[0]),
                (from_high, layers.at[1]),
                (from_left, slabs.at[0]),
                (from_right, slabs.at[1]),
            )
        )
    ]
    lane = lax.broadcasted_iota(jnp.int32, (TW, TL), 1)
    first_lane, last_lane = lane == 0, lane == TL - 1

    def around_z(parts, distance, mask):
        rolled = [pltpu.roll(part, distance % TL, 1) for part in parts]
        return [jnp.where(mask, rolled[(h - distance) % halves], rolled[h]) for h in range(halves)]

    store = pltpu.make_async_copy(out, out_ref, sems.at[5])
    for copy in received + [load]:
        copy.start()
    yield
    for copy in received:
        copy.wait()
    wide[...] = layers[...].astype(jnp.float32)
    size = halves * rows
    for side, base in ((slabs.at[0], main - DEPTH), (slabs.at[1], main + nx)):
        for c in range(FIELDS + 1):
            for d in range(DEPTH):
                number = c * DEPTH + d
                block = side[number * size : (number + 1) * size, :].astype(jnp.float32)
                for h in range(halves):
                    begin[c, base + d, h] = block[h * rows : (h + 1) * rows] + CENTRE[c]

    def fill(x, _):
        for c in range(FIELDS + 1):
            for h in range(halves):
                begin[c, x + main, h, ny:rows, :] = ghost_rows(low, high, c, h, x, TIME_STEP)
        return 0

    lax.fori_loop(0, nx, fill, 0)
    load.wait()

    for section, (alpha, beta) in enumerate(SECTIONS):
        last = section == len(SECTIONS) - 1
        source, target = ((begin, state_one), (state_one, state_two), (state_two, out))[section]
        tiles = (ny if last else rows) // TW

        def step(i, turn):
            now, one, two, three = (turn % RINGS, *((turn - k) % RINGS for k in (1, 2, 3)))
            x = i - LAG
            for q in range(rows // TW):
                at = slice(q * TW, (q + 1) * TW)
                base = TW + q * TW
                here, after, before = (slice(base + k, base + k + TW) for k in (0, 1, -1))
                if q < tiles:
                    along_z = []
                    for b in range(FIELDS):
                        up = [up_z[two][b, h, at, :] for h in range(halves)]
                        down = [down_z[two][b, h, at, :] for h in range(halves)]
                        up = around_z(up, -1, last_lane)
                        down = around_z(down, 1, first_lane)
                        along_z.append([up[h] + down[h] for h in range(halves)])
                for h in range(halves):
                    for b in range(FIELDS):
                        if q >= tiles:
                            break
                        k = b - 1
                        rate = along_z[b][h] + (
                            (flux_x[three][b, h, at, :] - flux_x[one][b, h, at, :])
                            + (flux_y[two][b, h, before, :] - flux_y[two][b, h, after, :])
                        )
                        if b > 0:
                            sum_x = f_s[three][k, h, here, :] + f_s[one][k, h, here, :]
                            sum_y = f_s[two][k, h, before, :] + f_s[two][k, h, after, :]
                            rate = rate + ((sum_x + sum_y) - 6.0 * f_s[two][k, h, here, :])
                        moved = source[b, x, h, at, :] + begin[FIELDS, x, h, at, :] * rate
                        if section > 0:
                            moved = alpha * begin[b, x, h, at, :] + beta * moved
                        if last:
                            place = jnp.maximum(x - main, 0)
                            out[b, place, at, h * TL : (h + 1) * TL] = moved
                        else:
                            target[b, x, h, at, :] = moved
                    f, flux = primitives([source[c, i, h, at, :] for c in range(FIELDS)])
                    wrap = None
                    if q == 0:
                        wrap = slice(TW + rows, 2 * TW + rows)
                    if (q + 1) * TW == rows:
                        wrap = slice(0, TW)
                    for b in range(FIELDS):
                        if q < tiles:
                            flux_x[now][b, h, at, :] = flux[0][b]
                        flux_y[now][b, h, here, :] = flux[1][b]
                        if wrap is not None:
                            flux_y[now][b, h, wrap, :] = flux[1][b]
                        if b > 0:
                            f_s[now][b - 1, h, here, :] = f[b - 1]
                            if wrap is not None:
                                f_s[now][b - 1, h, wrap, :] = f[b - 1]
                    if q < tiles:
                        for b in range(FIELDS):
                            part = flux[2][b]
                            up_z[now][b, h, at, :] = f[b - 1] - part if b > 0 else -part
                            down_z[now][b, h, at, :] = f[b - 1] + part if b > 0 else part

        reach = DEPTH - 1 - section
        stop = main + nx + reach + LAG
        turns = -(-(nx + 2 * reach + LAG + 1) // RINGS)

        def body(j, _):
            for turn in range(RINGS):
                step(stop - turns * RINGS + j * RINGS + turn, turn)
            return 0

        lax.fori_loop(0, turns, body, 0)

    store.start()
    yield
    store.wait()
    yield


def find(table, count, slots, block):
    where_j, where_t = jnp.int32(0), jnp.int32(0)
    for j in range(count):
        for t in range(slots):
            hit = table[j * RING + 2 + t] == block
            where_j = jnp.where(hit, j, where_j)
            where_t = jnp.where(hit, t, where_t)
    return where_j, where_t


def pack_kernel(count, slots, refs):
    table, block_faces = refs[:2]
    held = refs[2 : 2 + count // 2]
    packed, sems = refs[4 + count // 2 :]
    for finish in (False, True):
        pack(count, slots, table, block_faces, held, packed, sems, finish)


def pack(count, slots, table, block_faces, held, packed, sems, finish):
    me = lax.axis_index("gy")
    offset = jnp.where(lax.rem(me, 2) == 1, 1, count - 1)
    for s in range(slots):
        block = table[offset * RING + 2 + s]

        @pl.when(block >= 0)
        def _():
            for side in range(2):
                j, t = find(table, count, slots, block_faces[side, block])
                number = s * 2 + side
                for m in range(count // 2):

                    @pl.when(j == 2 * m)
                    def _():
                        copy = pltpu.make_async_copy(
                            held[m].at[t * 2 + 1 - side], packed.at[number], sems.at[number]
                        )
                        if finish:
                            copy.wait()
                        else:
                            copy.start()


def near_sections(count, slots, dims, edges, inputs, out_ref, scratch):
    per_slot, around, normal = dims
    table, block_faces, slot_ref, near_ref, metric_ref = inputs[:5]
    parcels, rest = inputs[5 : 5 + count], inputs[5 + count :]
    if edges:
        held, packed, main_ref = rest[: count // 2], rest[count // 2], rest[count // 2 + 1]
    own = 2 * TW if edges else around
    rows = own + RING if edges else own
    begins, metrics, state_one, state_two, square, coeff, hold, out, along = scratch[:9]
    tile_buf, in_sems, out_sems, tile_sems = scratch[9:13]
    rings = scratch[13:37]
    flux_n, flux_a, f_s = rings[:4], rings[4:8], rings[8:12]
    up_s, down_s, own_s = rings[12:16], rings[16:20], rings[20:24]
    if edges:
        ghost, face_buf, main_buf, face_sems, main_sems = scratch[37:]
    lines = FIELDS * TW * TW
    wall = (-1.0, 1.0, 1.0, 1.0, -1.0)
    mirror = (-1.0, -1.0, -1.0, 1.0)
    pieces = ((0, 0), (around - TW, TW)) if edges else ((0, 0),)
    piece = TW if edges else around

    def loads(s):
        side = lax.rem(s, 2)
        return [
            pltpu.make_async_copy(
                ref.at[s, :, :, pl.ds(source, piece), :],
                buf.at[side, :, :, pl.ds(target, piece), :],
                in_sems.at[k, p, side],
            )
            for k, (ref, buf) in enumerate(((near_ref, begins), (metric_ref, metrics)))
            for p, (source, target) in enumerate(pieces)
        ]

    def main_loads(s):
        return [
            pltpu.make_async_copy(
                main_ref.at[s, :, :, pl.ds(source, TW), :],
                main_buf.at[s, :, :, pl.ds(target, TW), :],
                main_sems.at[s, p],
            )
            for p, (source, target) in enumerate(pieces)
        ]

    def stores(s):
        return [
            pltpu.make_async_copy(
                out.at[s, :, :, pl.ds(target, piece), :],
                out_ref.at[s, :, :, pl.ds(source, piece), :],
                out_sems.at[s, p],
            )
            for p, (source, target) in enumerate(pieces)
        ]

    def start_loads(s):
        @pl.when(slot_ref[s] >= 0)
        def _():
            for copy in loads(s):
                copy.start()

    start_loads(0)
    lane = lax.broadcasted_iota(jnp.int32, (rows, TL), 1)
    tile_loads = [
        pltpu.make_async_copy(
            parcels[j].at[pl.ds(lines, lines), :], tile_buf.at[j], tile_sems.at[j]
        )
        for j in range(count)
    ]
    for copy in tile_loads:
        copy.start()

    def face_loads(s):
        for side in range(2):
            j, t = find(table, count, slots, block_faces[side, slot_ref[s]])
            target, sem = face_buf.at[s, side], face_sems.at[s, side]
            for m in range(count // 2):

                @pl.when(j == 2 * m)
                def _():
                    pltpu.make_async_copy(held[m].at[t * 2 + 1 - side], target, sem).start()

            @pl.when(lax.rem(j, 2) == 1)
            def _():
                pltpu.make_async_copy(packed.at[s * 2 + side], target, sem).start()

    if edges:
        for s in range(slots):

            @pl.when(slot_ref[s] >= 0)
            def _():
                face_loads(s)
                for copy in main_loads(s):
                    copy.start()

    yield
    row = lax.broadcasted_iota(jnp.int32, (RING, TL), 0)

    def take_ghosts(s, begin, metric):
        for side in range(2):
            pltpu.make_async_copy(
                packed.at[0], face_buf.at[s, side], face_sems.at[s, side]
            ).wait()
            ghost[side] = face_buf[s, side].astype(jnp.float32)

        def ghost_tile(number, layers, i, fill, centre):
            tile = jnp.full((RING, TL), fill, jnp.float32)
            for d in range(layers):
                at = (number + d) * TW + i
                line = jnp.broadcast_to(ghost[1, at : at + 1, :] + centre, (RING, TL))
                tile = jnp.where(row == d, line, tile)
                line = jnp.broadcast_to(ghost[0, at : at + 1, :] + centre, (RING, TL))
                tile = jnp.where(row == RING - layers + d, line, tile)
            return tile

        step = DEPTH - 1
        for i in range(normal):
            for c in range(FIELDS):
                begin[c, i, own:rows, :] = ghost_tile(
                    c * DEPTH, DEPTH, i, QUIET_STATE[c], CENTRE[c]
                )
            for a in range(3):
                metric[a, i, own:rows, :] = ghost_tile(
                    FIELDS * DEPTH + a * step, step, i, 1.0, 0.0
                )
        last_layer = (FACE_LAYERS - 1) * TW
        hold[own:rows, :] = TIME_STEP * jnp.where(
            row < RING // 2,
            ghost[1, last_layer : last_layer + TW, :],
            ghost[0, last_layer : last_layer + TW, :],
        )

    def slot_work(s, _):
        begin, metric = begins.at[lax.rem(s, 2)], metrics.at[lax.rem(s, 2)]

        @pl.when(s + 1 < slots)
        def _():
            start_loads(jnp.minimum(s + 1, slots - 1))

        if not edges:

            @pl.when(slot_ref[s] < 0)
            def _():
                out[s] = jnp.zeros(out.shape[1:], jnp.float32)

        @pl.when(slot_ref[s] >= 0)
        def _():
            if edges:
                take_ghosts(s, begin, metric)
            hold[0:own, :] = jnp.full((own, TL), TIME_STEP, jnp.float32)
            for copy in loads(s):
                copy.wait()
            if edges:
                for copy in main_loads(s):
                    copy.wait()

            for j in range(count):
                tile = table[j * RING + 1]
                number = tile % per_slot
                mine = (tile >= 0) & (tile // per_slot == s)
                if edges:
                    mine = mine & ((number == 0) | (number == per_slot - 1))
                    number = jnp.where(number == 0, 0, 1)

                @pl.when(mine)
                def _():
                    q = aligned(number, TW)
                    for c in range(FIELDS):
                        for i in range(0, TW, 2):
                            start = (c * TW + i) * TW
                            pair = tile_buf[j, start : start + 2 * TW, :].astype(jnp.float32)
                            begin[c, i, pl.ds(q, TW), :] = pair[:TW]
                            begin[c, i + 1, pl.ds(q, TW), :] = pair[TW:]
                    hold[pl.ds(q, TW), :] = jnp.zeros((TW, TL), jnp.float32)

            def prepare(i, _):
                squares = [metric[a, i] * metric[a, i] for a in range(3)]
                for a in range(2):
                    square[a, i] = squares[a]
                total = -2.0 * ((squares[0] + squares[1]) + squares[2])
                at_end = (lane == 0) | (lane == TL - 1)
                coeff[i] = jnp.where(at_end, total + squares[2], total)
                g = metric[2, i]
                along[0, i] = jnp.where(lane == 0, 0.0, pltpu.roll(g, 1, 1))
                along[1, i] = jnp.where(lane == TL - 1, 0.0, pltpu.roll(g, TL - 1, 1))
                along[2, i] = jnp.where(lane == 0, g, jnp.where(lane == TL - 1, -g, 0.0))
                return 0

            lax.fori_loop(0, normal, prepare, 0)

            for section, (alpha, beta) in enumerate(SECTIONS):
                last = section == len(SECTIONS) - 1
                source = (begin, state_one, state_two)[section]
                target = (state_one, state_two, out)[section]
                tiles = (own if last else rows) // TW

                def advance(x, q):
                    at = slice(q * TW, (q + 1) * TW)
                    base = TW + q * TW
                    here, after, before = (slice(base + k, base + k + TW) for k in (0, 1, -1))
                    mid, low = x % RINGS, (x - 1) % RINGS
                    high = (x + 1) % RINGS
                    g = [metric[a, x, at, :] for a in range(2)]
                    g2 = [square[a, x, at, :] for a in range(2)]
                    center = coeff[x, at, :]
                    for b in range(FIELDS):
                        k = b - 1
                        rate = pltpu.roll(up_s[mid][b, at, :], TL - 1, 1)
                        rate = rate + pltpu.roll(down_s[mid][b, at, :], 1, 1)
                        rate = rate + own_s[mid][b, at, :]
                        rate = rate + g[0] * (flux_n[low][b, at, :] - flux_n[high][b, at, :])
                        rate = rate + g[1] * (
                            flux_a[mid][b, before, :] - flux_a[mid][b, after, :]
                        )
                        if b > 0:
                            rate = rate + g2[0] * (f_s[low][k, here, :] + f_s[high][k, here, :])
                            rate = rate + g2[1] * (
                                f_s[mid][k, before, :] + f_s[mid][k, after, :]
                            )
                            rate = rate + center * f_s[mid][k, here, :]
                        moved = source[b, x, at, :] + hold[at, :] * rate
                        if section > 0:
                            moved = alpha * begin[b, x, at, :] + beta * moved
                        if last and edges:
                            right = row < DEPTH if q == 0 else row >= TW - DEPTH
                            moved = jnp.where(right, moved, main_buf[s, b, x, at, :])
                        if last:
                            out[s, b, x, at, :] = moved
                        else:
                            target[b, x, at, :] = moved

                def work(i, q):
                    at = slice(q * TW, (q + 1) * TW)
                    base = TW + q * TW
                    here = slice(base, base + TW)
                    now = i % RINGS
                    f, flux = primitives([source[c, i, at, :] for c in range(FIELDS)])
                    wrap = None
                    if q == 0:
                        wrap = slice(TW + rows, 2 * TW + rows)
                    if base == rows:
                        wrap = slice(0, TW)
                    for b in range(FIELDS):
                        if q < tiles:
                            flux_n[now][b, at, :] = flux[0][b]
                            if i == 0:
                                flux_n[now - 1][b, at, :] = wall[b] * flux[0][b]
                            if i == normal - 1:
                                flux_n[(now + 1) % RINGS][b, at, :] = flux[0][b]
                        flux_a[now][b, here, :] = flux[1][b]
                        if wrap is not None:
                            flux_a[now][b, wrap, :] = flux[1][b]
                        if b > 0:
                            f_s[now][b - 1, here, :] = f[b - 1]
                            if wrap is not None:
                                f_s[now][b - 1, wrap, :] = f[b - 1]
                            if i == 0:
                                f_s[now - 1][b - 1, here, :] = mirror[b - 1] * f[b - 1]
                            if i == normal - 1:
                                f_s[(now + 1) % RINGS][b - 1, here, :] = f[b - 1]
                    if q < tiles:
                        g_up, g_down = along[0, i, at, :], along[1, i, at, :]
                        g_own = along[2, i, at, :]
                        for b in range(FIELDS):
                            part = flux[2][b]
                            if b > 0:
                                up_s[now][b, at, :] = g_up * (g_up * f[b - 1] - part)
                                down_s[now][b, at, :] = g_down * (g_down * f[b - 1] + part)
                            else:
                                up_s[now][b, at, :] = -(g_up * part)
                                down_s[now][b, at, :] = g_down * part
                            own_s[now][b, at, :] = g_own * part

                for i in range(normal + LAG):
                    for q in range(rows // TW):
                        if i >= LAG and q < tiles:
                            advance(i - LAG, q)
                        if i < normal:
                            work(i, q)

        def send_out():
            for copy in stores(s):
                copy.start()

        if edges:
            pl.when(slot_ref[s] >= 0)(send_out)
        else:
            send_out()
        return 0

    for copy in tile_loads:
        copy.wait()
    lax.fori_loop(0, slots, slot_work, 0)
    yield
    for s in range(slots):

        def end_out():
            for copy in stores(s):
                copy.wait()

        if edges:
            pl.when(slot_ref[s] >= 0)(end_out)
        else:
            end_out()
    yield


def near_kernel(count, slots, dims, refs):
    inputs, (out_ref, token) = refs[: 5 + count], refs[6 + count : 8 + count]
    token[...] = jnp.zeros(token.shape, jnp.float32)
    for _ in near_sections(count, slots, dims, False, inputs, out_ref, refs[8 + count :]):
        pass


def edge_kernel(count, slots, dims, refs):
    size = 5 + count + count // 2 + 2
    out_ref, scratch = refs[size + 1], refs[size + 2 :]
    for _ in near_sections(count, slots, dims, True, refs[:size], out_ref, scratch):
        pass


def off_kernel(dims, refs):
    out_ref, token = refs[6:8]
    token[...] = jnp.zeros(token.shape, jnp.float32)
    for _ in off_sections(dims, refs[:5], out_ref, refs[8:]):
        pass


def packed_refs(kernel, *first):
    def body(*refs):
        kernel(*first, refs)

    return body


def off_buffers(dims, layer_shape, slab_shape):
    nx, ny, nz = dims
    halves, rows = nz // TL, ny + RING
    f32, half = jnp.float32, jnp.bfloat16
    slices = FRONT + nx + 2 * DEPTH + 2
    return (
        [
            VMEM((FIELDS, nx, ny, nz), f32),
            VMEM((2,) + layer_shape, half),
            VMEM((2,) + slab_shape, half),
            VMEM((2,) + layer_shape, f32),
            VMEM((FIELDS + 1, slices, halves, rows, TL), f32),
            VMEM((FIELDS, slices, halves, rows, TL), f32),
            VMEM((FIELDS, slices, halves, rows, TL), f32),
            pltpu.SemaphoreType.DMA((6,)),
        ]
        + [VMEM((FIELDS, halves, rows, TL), f32)] * RINGS
        + [VMEM((FIELDS, halves, rows + 2 * TW, TL), f32)] * RINGS
        + [VMEM((FIELDS - 1, halves, rows + 2 * TW, TL), f32)] * RINGS
        + [VMEM((FIELDS, halves, rows, TL), f32)] * RINGS * 2
    )


def near_buffers(count, slots, dims, edges):
    _, around, normal = dims
    f32, dma = jnp.float32, pltpu.SemaphoreType.DMA
    own = 2 * TW if edges else around
    rows = own + RING if edges else own
    pieces = 2 if edges else 1
    extra = []
    if edges:
        extra = [
            VMEM((2, FACE_ROWS, TL), f32),
            VMEM((slots, 2, FACE_ROWS, TL), jnp.bfloat16),
            VMEM((slots, FIELDS, normal, own, TL), f32),
            dma((slots, 2)),
            dma((slots, 2)),
        ]
    return (
        [
            VMEM((2, FIELDS, normal, rows, TL), f32),
            VMEM((2, 3, normal, rows, TL), f32),
            VMEM((FIELDS, normal, rows, TL), f32),
            VMEM((FIELDS, normal, rows, TL), f32),
            VMEM((2, normal, rows, TL), f32),
            VMEM((normal, rows, TL), f32),
            VMEM((rows, TL), f32),
            VMEM((slots, FIELDS, normal, own, TL), f32),
            VMEM((3, normal, rows, TL), f32),
            VMEM((count, FIELDS * TW * TW, TL), jnp.bfloat16),
            dma((2, pieces, 2)),
            dma((slots, pieces)),
            dma((count,)),
        ]
        + [VMEM((FIELDS, rows, TL), f32)] * RINGS
        + [VMEM((FIELDS, rows + 2 * TW, TL), f32)] * RINGS
        + [VMEM((FIELDS - 1, rows + 2 * TW, TL), f32)] * RINGS
        + [VMEM((FIELDS, rows, TL), f32)] * RINGS * 3
        + extra
    )


def ring(axis, distance):
    count = lax.axis_size(axis)
    return [(i, (i + distance) % count) for i in range(count)]


def send(value, axis, distance):
    return lax.ppermute(value, axis, ring(axis, distance))


def local(
    off_state,
    near_state,
    near_metric,
    slot_block,
    block_faces,
    fringe_in,
    fringe_in_maps,
    fringe_out,
    fringe_out_maps,
):
    count = lax.axis_size("gy")
    slots, _, normal, around, span = near_state.shape
    _, nx, ny, nz = off_state.shape
    rows_here = fringe_in.shape[1]
    per_slot = around // TW
    lines = FIELDS * TW * TW
    half, f32 = jnp.bfloat16, jnp.float32
    shape = jax.ShapeDtypeStruct
    block_faces = block_faces.T
    tile_buf = VMEM((count, FIELDS, TW, TW, TL), f32)
    map_buf = VMEM((count, TL, TL), half)

    parcels = pl.pallas_call(
        packed_refs(
            interp_kernel, count, slots, (rows_here, per_slot, ny // TW, nz // TL)
        ),
        out_shape=[shape((2 * lines + META, TL), half)] * count,
        in_specs=[smem_spec()] * 3 + [any_spec()] * 4,
        out_specs=[vmem_spec()] * count,
        scratch_shapes=[
            tile_buf,
            tile_buf,
            map_buf,
            map_buf,
            pltpu.SemaphoreType.DMA((4, count)),
        ],
        compiler_params=params(VMEM_MIB),
        cost_estimate=cost(2e8, 6e6),
        name="interp",
    )(fringe_in, fringe_out, slot_block, off_state, near_state, fringe_in_maps, fringe_out_maps)
    dma = pltpu.SemaphoreType.DMA
    planes = (FIELDS + 1) * DEPTH
    halves = nz // TL
    layer_shape = (planes, halves, nx, TL)
    base_layers, base_faces, base_placed = pl.pallas_call(
        packed_refs(base_kernel, slots, (around, nx, ny, nz)),
        out_shape=[
            shape((2,) + layer_shape, f32),
            shape((2 * slots, FACE_ROWS, TL), f32),
            shape((FIELDS + 1, nx, halves, ny, TL), f32),
        ],
        in_specs=[vmem_spec()] + [any_spec()] * 2,
        out_specs=[vmem_spec()] * 3,
        scratch_shapes=[
            VMEM((2, slots, FIELDS, normal, TW, TL), f32),
            VMEM((2, slots, 3, normal, TW, TL), f32),
            dma((2, 2)),
        ],
        compiler_params=params(VMEM_MIB),
        cost_estimate=cost(1e7, 2e7),
        name="base",
    )(off_state, near_state, near_metric)

    parcels = [parcels[0]] + [send(parcels[j], "gy", j) for j in range(1, count)]

    y_low, y_high, faces, table, placed = pl.pallas_call(
        packed_refs(patch_kernel, count, per_slot, (nx, ny, nz)),
        out_shape=[
            shape(layer_shape, half),
            shape(layer_shape, half),
            shape((2 * slots, FACE_ROWS, TL), half),
            shape((count * RING,), jnp.int32),
            shape(base_placed.shape, f32),
        ],
        in_specs=[any_spec()] * (count + 3),
        out_specs=[vmem_spec()] * 3 + [smem_spec(), any_spec()],
        input_output_aliases={count + 2: 4},
        scratch_shapes=[
            VMEM((2,) + layer_shape, f32),
            VMEM((2 * slots, FACE_ROWS, TL), f32),
            VMEM((count, 2 * lines + META, TL), half),
            VMEM((count, lines, TL), f32),
            VMEM((lines, TL), f32),
            VMEM((TW, TW, TL), f32),
            VMEM((count * META, TL), jnp.int32),
            SMEM((count * META, TL), jnp.int32),
            dma((2 * count + 3,)),
            dma((2, count)),
        ],
        compiler_params=params(VMEM_MIB),
        cost_estimate=cost(1e7, 8e6),
        name="patch",
    )(*parcels, base_layers, base_faces, base_placed)

    held = [faces] + [send(faces, "gy", 2 * m) for m in range(1, count // 2)]
    from_low = send(y_high, "gy", 1)
    from_high = send(y_low, "gy", count - 1)

    near_dims, off_dims = (per_slot, around, normal), (nx, ny, nz)
    near_inputs = (table, block_faces, slot_block, near_state, near_metric, *parcels)
    token_shape = shape((RING, TL), f32)

    near_main, token = pl.pallas_call(
        packed_refs(near_kernel, count, slots, near_dims),
        out_shape=[shape(near_state.shape, f32), token_shape],
        in_specs=[smem_spec()] * 3 + [any_spec()] * (2 + count + 1),
        out_specs=[any_spec(), vmem_spec()],
        scratch_shapes=near_buffers(count, slots, near_dims, False),
        compiler_params=params(56),
        cost_estimate=cost(1e8, 5e7),
        name="near_sections",
    )(*near_inputs, faces)

    x_low, x_high = pl.pallas_call(
        packed_refs(slab_kernel, off_dims),
        out_shape=[shape((planes * halves * (ny + RING), TL), half)] * 2,
        in_specs=[any_spec()] * 4,
        out_specs=[vmem_spec()] * 2,
        scratch_shapes=[
            VMEM((2,) + layer_shape, half),
            VMEM((2,) + layer_shape, f32),
            VMEM((2, FIELDS + 1, DEPTH, halves, ny, TL), f32),
            dma((4,)),
        ],
        compiler_params=params(8),
        cost_estimate=cost(1e6, 4e6),
        name="slabs",
    )(placed, from_low, from_high, token)
    from_left = send(x_high, "gx", 1)
    from_right = send(x_low, "gx", lax.axis_size("gx") - 1)

    packed_here = pl.pallas_call(
        packed_refs(pack_kernel, count, slots),
        out_shape=shape((2 * slots, FACE_ROWS, TL), half),
        in_specs=[smem_spec()] * 2 + [any_spec()] * (count // 2 + 2),
        out_specs=vmem_spec(),
        scratch_shapes=[dma((2 * slots,))],
        compiler_params=params(4),
        cost_estimate=cost(1e5, 2e6),
        name="pack",
    )(table, block_faces, *held, from_left, from_right)
    packed = lax.ppermute(packed_here, "gy", [(i, i ^ 1) for i in range(count)])

    off_next, token = pl.pallas_call(
        packed_refs(off_kernel, off_dims),
        out_shape=[shape(off_state.shape, f32), token_shape],
        in_specs=[any_spec()] * 6,
        out_specs=[any_spec(), vmem_spec()],
        scratch_shapes=off_buffers(off_dims, layer_shape, x_low.shape),
        compiler_params=params(VMEM_MIB),
        cost_estimate=cost(1e8, 5e7),
        name="off_sections",
    )(placed, from_low, from_high, from_left, from_right, packed_here)

    number = len(near_inputs) + count // 2 + 1
    near_next = pl.pallas_call(
        packed_refs(edge_kernel, count, slots, near_dims),
        out_shape=shape(near_state.shape, f32),
        in_specs=[smem_spec()] * 3 + [any_spec()] * (number - 2 + 1),
        out_specs=any_spec(),
        input_output_aliases={number: 0},
        scratch_shapes=near_buffers(count, slots, near_dims, True),
        compiler_params=params(VMEM_MIB),
        cost_estimate=cost(1e8, 5e7),
        name="near_edges",
    )(*near_inputs, *held, packed, near_main, token)
    return off_next, near_next


def solution(mesh):
    in_specs = (
        P(None, "gx", "gy", None),
        P(("gx", "gy"), None, None, None, None),
        P(("gx", "gy"), None, None, None, None),
        P(("gx", "gy")),
        P(),
        P(None, ("gx", "gy")),
        P(("gx", "gy"), None, None),
        P(None, ("gx", "gy")),
        P(("gx", "gy"), None, None),
    )
    out_specs = (P(None, "gx", "gy", None), P(("gx", "gy"), None, None, None, None))
    return jax.shard_map(local, mesh=mesh, in_specs=in_specs, out_specs=out_specs, check_vma=False)
```
